256 devices in a mesh: wide: 32 (over z, y_lo, core), narrow: 8 (over y_hi, x).
Axes of the slice: x: 4, y: 4 (y_hi: 2, y_lo: 2; y = y_hi * 2 + y_lo), z: 8, core: 2. Of those that a mesh axis runs over, the one named last changes fastest.
Arguments:
- video: bfloat16 [128, 16, 64, 1024], P('wide', 'narrow'), may hold values from -15 to 15
- w_qkv: bfloat16 [1024, 3072], replicated, may hold values from -0.1875 to 0.1875
- w_out: bfloat16 [1024, 1024], replicated, may hold values from -0.1875 to 0.1875
- w_proj: bfloat16 [1024, 768], replicated, may hold values from -0.1875 to 0.1875
- captions: bfloat16 [4096, 768], P(('wide', 'narrow')), may hold values from -330 to 330
- positive: int32 [128], P('wide'), may hold values from 0 to 4095
Outputs:
- clip_grad: float32 [128, 768], P('wide')
- caption_grad: float32 [4096, 768], P(('wide', 'narrow'))
The draws below stay inside these ranges and needn't reach their ends.
All inputs are finite; a program needn't handle non-finite values.
Results may differ from the reference program's by a relative error of at most 0.0085.
Values may be sent and summed in bfloat16 or wider, within the bound.
No kernel may reach another device: no remote copies, remote signals or barrier semaphores. Data moves between devices by JAX's collectives and lax.ppermute only.
A program may use at most 64 MiB of HBM per device.

```python
import jax
import jax.numpy as jnp
from jax import lax

D = 1024
HEADS = 16
E = 768
FRAMES = 16
SPATIAL = 64
CLIPS = 128
CAPTIONS = 4096


def draw_video(key, part):
    key = jax.random.fold_in(key, 11)
    first = jax.random.fold_in(key, 0)
    shape = (CLIPS, FRAMES, SPATIAL, D)
    steps = jnp.arange(FRAMES, dtype=jnp.float32) / max(FRAMES - 1, 1)
    frame_scale = (3.0 ** steps).reshape(1, FRAMES, 1, 1)
    base = jnp.clip(jax.random.normal(first, shape, jnp.float32), -5.0, 5.0)
    return (base * frame_scale).astype(jnp.bfloat16)


def draw_captions(key, part):
    key = jax.random.fold_in(key, 23)
    first, second, third = jax.random.split(key, 3)
    row_scale = jnp.exp(jax.random.uniform(second, (CAPTIONS, 1), jnp.float32, 0.0, 2.302585))
    col_scale = jnp.exp(jax.random.uniform(third, (1, E), jnp.float32, 0.0, 2.302585))
    base = jnp.clip(jax.random.normal(first, (CAPTIONS, E), jnp.float32), -3.3, 3.3)
    return (base * row_scale * col_scale).astype(jnp.bfloat16)


def with_ends(entries, key, smallest, top_value):
    longest = entries.shape.index(max(entries.shape))
    spots = []
    for shift in (0, 1):
        where = [jax.random.randint(jax.random.fold_in(key, axis), (), 0, length) for axis, length in enumerate(entries.shape)]
        where[longest] = (where[longest] + shift) % entries.shape[longest]
        spots.append(tuple(where))
    return entries.at[spots[0]].set(smallest).at[spots[1]].set(top_value)


def bell_draw(rng, extent, deviation, bound, kind=jnp.bfloat16):
    drawn = jax.random.normal(rng, extent, jnp.float32) * deviation
    return jnp.minimum(jnp.maximum(drawn, -bound), bound).astype(kind)


def setup_inputs(seed: int = 0) -> dict:
    key_list = jax.random.split(jax.random.key(seed), 7)
    video = draw_video(jax.random.fold_in(key_list[6], 71), 0)
    w_qkv = bell_draw(key_list[1], (D, 3 * D), D ** -0.5, 0.1875)
    w_out = bell_draw(key_list[2], (D, D), D ** -0.5, 0.1875)
    w_proj = bell_draw(key_list[3], (D, E), D ** -0.5, 0.1875)
    captions = draw_captions(jax.random.fold_in(key_list[6], 71), 0)
    positive = with_ends(jax.random.randint(key_list[5], (CLIPS,), 0, CAPTIONS), jax.random.fold_in(key_list[5], 1), 0, CAPTIONS - 1).astype(jnp.int32)
    return dict(video=video, w_qkv=w_qkv, w_out=w_out, w_proj=w_proj, captions=captions, positive=positive)


TEMP = 10.0
BIAS = -2.0
EPS = 1e-06

def clip_layer(tokens, w_qkv, w_out):
    rows = tokens.reshape(FRAMES * SPATIAL, D)
    qkv = jnp.dot(rows, w_qkv, preferred_element_type=jnp.float32).astype(jnp.bfloat16)
    qkv = qkv.reshape(FRAMES, SPATIAL, 3, HEADS, D // HEADS)
    query = qkv[:, :, 0].astype(jnp.float32)
    keys = qkv[:, :, 1].astype(jnp.float32)
    values = qkv[:, :, 2].astype(jnp.float32)
    scores = jnp.einsum('fshd,gshd->shfg', query, keys) * (1.0 / jnp.sqrt(jnp.float32(D // HEADS)))
    top = lax.optimization_barrier(jnp.max(scores, axis=-1, keepdims=True))
    expo = jnp.exp(scores - top)
    probs = (expo / lax.optimization_barrier(jnp.sum(expo, axis=-1, keepdims=True))).astype(jnp.bfloat16)
    mixed = jnp.einsum('shfg,gshd->fshd', probs.astype(jnp.float32), values)
    mixed = mixed.astype(jnp.bfloat16).reshape(FRAMES * SPATIAL, D)
    layer_out = rows.astype(jnp.float32) + jnp.dot(mixed, w_out, preferred_element_type=jnp.float32)
    return lax.optimization_barrier(jnp.sum(layer_out, axis=0))

def reference(video, w_qkv, w_out, w_proj, captions, positive):
    pooled = lax.map(lambda tokens: clip_layer(tokens, w_qkv, w_out), video) / (FRAMES * SPATIAL)
    embed = jnp.dot(pooled, w_proj.astype(jnp.float32), precision=lax.Precision.HIGHEST)
    length = jnp.sqrt(lax.optimization_barrier(jnp.sum(embed * embed, axis=-1, keepdims=True)) + EPS)
    unit = embed / length
    cap = captions.astype(jnp.float32)
    cap_len = jnp.sqrt(lax.optimization_barrier(jnp.sum(cap * cap, axis=-1, keepdims=True)) + EPS)
    cap_unit = cap / cap_len
    logits = TEMP * jnp.dot(unit, cap_unit.T, precision=lax.Precision.HIGHEST) + BIAS
    index = jnp.arange(CAPTIONS, dtype=jnp.int32)
    sign = jnp.where(index[None, :] == positive[:, None], 1.0, -1.0).astype(logits.dtype)
    weight = -sign * jax.nn.sigmoid(-sign * logits)
    grad_unit = TEMP * jnp.dot(weight, cap_unit, precision=lax.Precision.HIGHEST)
    grad_cap = TEMP * jnp.dot(weight.T, unit, precision=lax.Precision.HIGHEST)
    clip_grad = (grad_unit - unit * lax.optimization_barrier(jnp.sum(unit * grad_unit, axis=-1, keepdims=True))) / length
    caption_grad = (grad_cap - cap_unit * lax.optimization_barrier(jnp.sum(cap_unit * grad_cap, axis=-1, keepdims=True))) / cap_len
    return (clip_grad, caption_grad)
```

```python
import jax
import jax.numpy as jnp
from jax import lax
from jax.experimental import pallas as pl
from jax.experimental.pallas import tpu as pltpu
from jax.sharding import PartitionSpec as P

D = 1024
E = 768
HEADS = 16
HEAD = D // HEADS
FRAMES = 16
SPATIAL = 64
TOKENS = FRAMES * SPATIAL
LANES = 128
GROUP = 4
WIDTH = GROUP * HEAD
BLOCKS = 4
ROWS = FRAMES * 8

TEMP = 10.0
BIAS = -2.0
EPS = 1e-06
LOG2E = 1.4426950408889634

F32 = jnp.float32
BF16 = jnp.bfloat16


def dot(a, b):
    return jnp.dot(a, b, preferred_element_type=F32)


def dot_t(a, b):
    return lax.dot_general(a, b, (((1,), (1,)), ((), ())), preferred_element_type=F32)


def parts_of(value, count):
    terms = []
    for _ in range(count):
        term = value.astype(BF16)
        terms.append(term)
        value = value - term.astype(F32)
    return terms


def temporal_kernel(x_ref, wqkv_hbm, wout_hbm, wproj_hbm, out_ref, wqkv, wout, wproj, weights, sems):
    copies = []
    for j in range(HEADS // GROUP):
        for k in range(2):
            cols = pl.ds(k * D + j * WIDTH, WIDTH)
            copies.append(pltpu.make_async_copy(wqkv_hbm.at[:, cols], wqkv.at[:, cols], sems.at[len(copies)]))
    cols = pl.ds(2 * D, D)
    copies.append(pltpu.make_async_copy(wqkv_hbm.at[:, cols], wqkv.at[:, cols], sems.at[len(copies)]))
    copies.append(pltpu.make_async_copy(wout_hbm, wout, sems.at[len(copies)]))
    copies.append(pltpu.make_async_copy(wproj_hbm, wproj, sems.at[len(copies)]))
    for copy in copies:
        copy.start()
    x = jnp.concatenate([x_ref[:, 16 * b : 16 * b + 16, :].reshape(ROWS, D) for b in range(BLOCKS)], axis=0)
    lane = lax.broadcasted_iota(jnp.int32, (ROWS, WIDTH), 1) // HEAD
    same = lax.broadcasted_iota(jnp.int32, (8, ROWS), 0) == lax.broadcasted_iota(jnp.int32, (8, ROWS), 1) % 8
    ones = jnp.ones((8, ROWS), BF16)
    for j in range(HEADS // GROUP):
        copies[2 * j].wait()
        query = dot(x, wqkv[:, j * WIDTH : (j + 1) * WIDTH]).astype(BF16)
        copies[2 * j + 1].wait()
        keys = dot(x, wqkv[:, D + j * WIDTH : D + (j + 1) * WIDTH]).astype(BF16)
        for b in range(BLOCKS):
            q = query[b * ROWS : (b + 1) * ROWS]
            k = keys[b * ROWS : (b + 1) * ROWS]
            split = jnp.concatenate([jnp.where(lane == h, k, jnp.zeros_like(k)) for h in range(GROUP)], axis=0)
            scores = dot_t(split, q).reshape(GROUP, FRAMES, 8, ROWS)
            top = jnp.max(scores, axis=1, keepdims=True)
            expo = jnp.exp2((scores - top) * (HEAD**-0.5 * LOG2E))
            total = jnp.sum(expo, axis=1, keepdims=True)
            probs = expo * jnp.where(same, 1.0 / total, 0.0)
            row = dot_t(ones, probs.astype(BF16).reshape(GROUP * ROWS, ROWS))
            for h in range(GROUP):
                weights[j * GROUP + h : j * GROUP + h + 1, b * ROWS : (b + 1) * ROWS] = row[:1, h * ROWS : (h + 1) * ROWS]
    left = parts_of(weights[...], 2) + [jnp.ones((HEADS, BLOCKS * ROWS), BF16)]
    sums = dot(jnp.concatenate(left, axis=0), x)
    heads = sums[:HEADS] + sums[HEADS : 2 * HEADS]
    rows = sums[2 * HEADS : 2 * HEADS + 1]
    copies[-3].wait()
    values = dot(jnp.concatenate(parts_of(heads, 2), axis=0), wqkv[:, 2 * D :])
    values = values[:HEADS] + values[HEADS:]
    own = lax.broadcasted_iota(jnp.int32, (HEADS, D), 0) == lax.broadcasted_iota(jnp.int32, (HEADS, D), 1) // HEAD
    mixed = jnp.sum(jnp.where(own, values, 0.0), axis=0, keepdims=True)
    copies[-2].wait()
    mixed = jnp.concatenate([jnp.broadcast_to(part, (8, D)) for part in parts_of(mixed, 2)], axis=0)
    layer = dot(mixed, wout[...])
    pooled = (rows + layer[:1] + layer[8:9]) * (1.0 / TOKENS)
    copies[-1].wait()
    pooled = jnp.concatenate([jnp.broadcast_to(part, (8, D)) for part in parts_of(pooled, 3)], axis=0)
    embed = dot(pooled, wproj[...])
    embed = embed[:8] + embed[8:16] + embed[16:24]
    for j in range(E // LANES):
        out_ref[:, j, :] = embed[:, j * LANES : (j + 1) * LANES]
    out_ref[:, E // LANES :, :] = jnp.zeros((8, 8 - E // LANES, LANES), F32)


def temporal(x, w_qkv, w_out, w_proj):
    anywhere = pl.BlockSpec(memory_space=pl.ANY)
    return pl.pallas_call(
        temporal_kernel,
        out_shape=jax.ShapeDtypeStruct((8, 8, LANES), F32),
        in_specs=[pl.BlockSpec(memory_space=pltpu.VMEM), anywhere, anywhere, anywhere],
        out_specs=pl.BlockSpec(memory_space=pltpu.VMEM),
        scratch_shapes=[
            pltpu.VMEM((D, 3 * D), BF16),
            pltpu.VMEM((D, D), BF16),
            pltpu.VMEM((D, E), BF16),
            pltpu.VMEM((HEADS, BLOCKS * ROWS), F32),
            pltpu.SemaphoreType.DMA((11,)),
        ],
        compiler_params=pltpu.CompilerParams(vmem_limit_bytes=40 << 20),
        cost_estimate=pl.CostEstimate(flops=3 << 30, bytes_accessed=11 << 20, transcendentals=0),
        name="temporal",
    )(x, w_qkv, w_out, w_proj)


def unit_kernel(parts_ref, positive_ref, unit_ref, length_ref, send_ref):
    for j in range(E // LANES):
        for c in range(4):
            unit_ref[c : c + 1, j * LANES : (j + 1) * LANES] = parts_ref[2 * c, j : j + 1, :] + parts_ref[2 * c + 1, j : j + 1, :]
    embed = unit_ref[...]
    length = jnp.sqrt(jnp.sum(embed * embed, axis=-1, keepdims=True) + EPS)
    unit = embed / length
    unit_ref[...] = unit
    length_ref[...] = jnp.broadcast_to(length, length_ref.shape)
    send_ref[:, :, :E] = jnp.broadcast_to(unit[None], (send_ref.shape[0], 4, E))
    send_ref[:, :, E:] = jnp.broadcast_to(positive_ref[...][None], (send_ref.shape[0], 4, LANES))


def make_units(parts, positive, copies):
    return pl.pallas_call(
        unit_kernel,
        out_shape=(
            jax.ShapeDtypeStruct((4, E), F32),
            jax.ShapeDtypeStruct((4, LANES), F32),
            jax.ShapeDtypeStruct((copies, 4, E + LANES), F32),
        ),
        name="units",
    )(parts, positive)


def row_lengths(cap):
    squares = cap.astype(F32)
    squares = squares * squares
    ones = jnp.ones((8, E), BF16)
    total = sum(dot_t(ones, part) for part in parts_of(squares, 2))
    return 1.0 / jnp.sqrt(total[:1] + EPS)


def slope(logits, hit):
    sign = jnp.where(hit, 1.0, -1.0)
    return -sign / (1.0 + jnp.exp(sign * logits))


def clip_kernel(unit_ref, cap_ref, ids_ref, positive_ref, out_ref):
    cap = cap_ref[...]
    scale = row_lengths(cap)
    logits = dot_t(jnp.concatenate(parts_of(unit_ref[...], 3), axis=0), cap)
    logits = (logits[:4] + logits[4:8] + logits[8:12]) * (TEMP * scale) + BIAS
    weight = slope(logits, ids_ref[...] == positive_ref[:, :1])
    grad = dot(jnp.concatenate(parts_of(weight * (TEMP * scale), 3), axis=0), cap)
    out_ref[...] = grad[:4] + grad[4:8] + grad[8:12]


def clip_part(unit, caps, ids, positive):
    return pl.pallas_call(
        clip_kernel,
        out_shape=jax.ShapeDtypeStruct((4, E), F32),
        compiler_params=pltpu.CompilerParams(vmem_limit_bytes=24 << 20),
        cost_estimate=pl.CostEstimate(flops=100 << 20, bytes_accessed=1 << 20, transcendentals=0),
        name="clip_part",
    )(unit, caps, ids, positive)


def caption_kernel(units_ref, other_ref, cap_ref, ids_ref, out_ref):
    cap = cap_ref[...].astype(F32)
    length = jnp.sqrt(jnp.sum(cap * cap, axis=-1, keepdims=True) + EPS)
    cap_unit = cap / length
    grad = jnp.zeros(cap.shape, F32)
    for ref in (units_ref, other_ref):
        rows = jnp.concatenate([ref[g] for g in range(ref.shape[0])], axis=0)
        unit = rows[:, :E]
        positive = rows[:, E:].T[:1]
        logits = TEMP * lax.dot_general(
            cap_unit, unit, (((1,), (1,)), ((), ())), precision=lax.Precision.HIGHEST, preferred_element_type=F32
        ) + BIAS
        weight = slope(logits, ids_ref[:, : rows.shape[0]] == positive)
        grad += TEMP * jnp.dot(weight, unit, precision=lax.Precision.HIGHEST, preferred_element_type=F32)
    out_ref[...] = (grad - cap_unit * jnp.sum(cap_unit * grad, axis=-1, keepdims=True)) / length


def caption_grads(units, other, captions, ids):
    return pl.pallas_call(
        caption_kernel,
        out_shape=jax.ShapeDtypeStruct(captions.shape, F32),
        compiler_params=pltpu.CompilerParams(vmem_limit_bytes=24 << 20),
        name="caption_grad",
    )(units, other, captions, ids)


def swapped(value, axis, bit):
    return lax.ppermute(value, axis, [(i, i ^ bit) for i in range(lax.axis_size(axis))])


def per_device(video, w_qkv, w_out, w_proj, captions, positive):
    wide = lax.axis_size("wide")
    narrow = lax.axis_size("narrow")
    rank_wide = lax.axis_index("wide")
    rank_narrow = lax.axis_index("narrow")
    cap_rows = captions.shape[0]
    chips = wide // 2
    same_core = [[2 * g + core for g in range(chips)] for core in range(2)]

    send = video.reshape(4, 2, 8, 8, D).transpose(0, 2, 1, 3, 4).reshape(8, 64, D)
    tokens = lax.all_to_all(send, "narrow", 0, 0, tiled=True)

    near = lax.all_to_all(
        jnp.broadcast_to(captions[None], (chips, cap_rows, E)), "wide", 0, 0, axis_index_groups=same_core, tiled=True
    )
    caps = jnp.concatenate([near, swapped(near, "wide", 1)], axis=0).reshape(wide * cap_rows, E)
    core = rank_wide % 2
    source = jnp.arange(wide, dtype=jnp.int32)
    source = jnp.where(source < chips, 2 * source + core, 2 * (source - chips) + 1 - core)
    cap_ids = (source[:, None] * narrow + rank_narrow) * cap_rows + jnp.arange(cap_rows, dtype=jnp.int32)[None]
    cap_ids = cap_ids.reshape(1, wide * cap_rows).astype(F32)
    own_ids = (rank_wide * narrow + rank_narrow) * cap_rows + jnp.arange(cap_rows, dtype=jnp.int32)
    own_ids = jnp.broadcast_to(own_ids.astype(F32)[:, None], (cap_rows, LANES))
    positive = jnp.broadcast_to(positive.astype(F32)[:, None], (4, LANES))

    parts = lax.all_to_all(temporal(tokens, w_qkv, w_out, w_proj), "narrow", 0, 0, tiled=True)
    unit, length, outgoing = make_units(parts, positive, chips)
    units = lax.all_to_all(outgoing, "wide", 0, 0, axis_index_groups=same_core, tiled=True)
    other = swapped(units, "wide", 1)
    caption_grad = caption_grads(units, other, captions, own_ids)

    grad_unit = clip_part(unit, caps, cap_ids, positive)
    for bit in (1, 2, 4):
        grad_unit = grad_unit + swapped(grad_unit, "narrow", bit)
    clip_grad = (grad_unit - unit * jnp.sum(unit * grad_unit, axis=-1, keepdims=True)) / length[:, :1]
    return (clip_grad, caption_grad)


def solution(mesh):
    in_specs = (
        P("wide", "narrow", None, None),
        P(),
        P(),
        P(),
        P(("wide", "narrow"), None),
        P("wide"),
    )
    out_specs = (P("wide", None), P(("wide", "narrow"), None))
    return jax.shard_map(
        per_device, mesh=mesh, in_specs=in_specs, out_specs=out_specs, check_vma=False
    )
```

```python
import jax
import jax.numpy as jnp
from jax import lax
from jax.experimental import pallas as pl
from jax.experimental.pallas import tpu as pltpu
from jax.sharding import PartitionSpec as P

D = 1024
E = 768
HEADS = 16
HEAD = D // HEADS
FRAMES = 16
SPATIAL = 64
TOKENS = FRAMES * SPATIAL
LANES = 128
GROUP = 4
WIDTH = GROUP * HEAD
BLOCKS = 4
ROWS = FRAMES * 8

TEMP = 10.0
BIAS = -2.0
EPS = 1e-06
LOG2E = 1.4426950408889634

ANYWHERE = pl.BlockSpec(memory_space=pl.ANY)
IN_VMEM = pl.BlockSpec(memory_space=pltpu.VMEM)

F32 = jnp.float32
BF16 = jnp.bfloat16


def dot(a, b):
    return jnp.dot(a, b, preferred_element_type=F32)


def dot_t(a, b):
    return lax.dot_general(a, b, (((1,), (1,)), ((), ())), preferred_element_type=F32)


def parts_of(value, count):
    terms = []
    for _ in range(count):
        term = value.astype(BF16)
        terms.append(term)
        value = value - term.astype(F32)
    return terms


def temporal_kernel(x_ref, wqkv_hbm, wout_hbm, wproj_hbm, out_ref, wqkv, wout, wproj, sems):
    copies = []

    def bring(source, target, columns):
        copy = pltpu.make_async_copy(source.at[:, columns], target.at[:, columns], sems.at[len(copies)])
        copy.start()
        copies.append(copy)

    for start, width in ((0, WIDTH), (WIDTH, D - WIDTH)):
        bring(wqkv_hbm, wqkv, pl.ds(start, width))
        bring(wqkv_hbm, wqkv, pl.ds(D + start, width))
    bring(wqkv_hbm, wqkv, pl.ds(2 * D, D))
    bring(wout_hbm, wout, pl.ds(0, D))
    bring(wproj_hbm, wproj, pl.ds(0, E))

    x = jnp.concatenate([x_ref[:, 16 * b : 16 * b + 16, :].reshape(ROWS, D) for b in range(BLOCKS)], axis=0)
    lane = lax.broadcasted_iota(jnp.int32, (ROWS, WIDTH), 1) // HEAD
    same = lax.broadcasted_iota(jnp.int32, (8, GROUP * ROWS), 0) == lax.broadcasted_iota(jnp.int32, (8, GROUP * ROWS), 1) % 8
    owner = lax.broadcasted_iota(jnp.int32, (GROUP * ROWS, LANES), 0) // ROWS
    column = lax.broadcasted_iota(jnp.int32, (GROUP * ROWS, LANES), 1)
    weights = jnp.zeros((BLOCKS * ROWS, LANES), F32)
    def project(j):
        query = dot(x, wqkv[:, j * WIDTH : (j + 1) * WIDTH]).astype(BF16)
        keys = dot(x, wqkv[:, D + j * WIDTH : D + (j + 1) * WIDTH]).astype(BF16)
        return query, keys

    def attend(query, keys, b):
        q = query[b * ROWS : (b + 1) * ROWS]
        k = keys[b * ROWS : (b + 1) * ROWS]
        split = jnp.concatenate([jnp.where(lane == h, q, jnp.zeros_like(q)) for h in range(GROUP)], axis=0)
        scores = dot_t(k, split).reshape(FRAMES, 8, GROUP * ROWS)
        top = jnp.max(scores, axis=0, keepdims=True)
        expo = jnp.exp2((scores - top) * (HEAD**-0.5 * LOG2E))
        total = jnp.sum(expo, axis=0, keepdims=True)
        return (expo * jnp.where(same, 1.0 / total, 0.0)).astype(BF16).reshape(ROWS, GROUP * ROWS)

    def place(j):
        return jnp.where(owner + j * GROUP == column, 1.0, 0.0).astype(BF16)

    copies[0].wait()
    copies[1].wait()
    ready = project(0)
    copies[2].wait()
    copies[3].wait()
    for j in range(HEADS // GROUP):
        current = ready
        if j + 1 < HEADS // GROUP:
            ready = project(j + 1)
        probs = [attend(*current, b) for b in range(BLOCKS)]
        weights += dot(jnp.concatenate(probs, axis=0), place(j))
    left = parts_of(weights.T[:HEADS], 2) + [jnp.ones((HEADS, BLOCKS * ROWS), BF16)]
    sums = dot(jnp.concatenate(left, axis=0), x)
    heads = sums[:HEADS] + sums[HEADS : 2 * HEADS]
    rows = sums[2 * HEADS : 2 * HEADS + 1]
    copies[-3].wait()
    values = dot(jnp.concatenate(parts_of(heads, 2), axis=0), wqkv[:, 2 * D :])
    values = values[:HEADS] + values[HEADS:]
    own = lax.broadcasted_iota(jnp.int32, (HEADS, D), 0) == lax.broadcasted_iota(jnp.int32, (HEADS, D), 1) // HEAD
    mixed = jnp.sum(jnp.where(own, values, 0.0), axis=0, keepdims=True)
    copies[-2].wait()
    mixed = jnp.concatenate([jnp.broadcast_to(part, (8, D)) for part in parts_of(mixed, 2)], axis=0)
    layer = dot(mixed, wout[...])
    pooled = (rows + layer[:1] + layer[8:9]) * (1.0 / TOKENS)
    copies[-1].wait()
    pooled = jnp.concatenate([jnp.broadcast_to(part, (8, D)) for part in parts_of(pooled, 3)], axis=0)
    embed = dot(pooled, wproj[...])
    embed = embed[:8] + embed[8:16] + embed[16:24]
    for j in range(E // LANES):
        out_ref[:, j, :] = embed[:, j * LANES : (j + 1) * LANES]
    out_ref[:, E // LANES :, :] = jnp.zeros((8, 8 - E // LANES, LANES), F32)


def temporal(x, w_qkv, w_out, w_proj):
    return pl.pallas_call(
        temporal_kernel,
        out_shape=jax.ShapeDtypeStruct((8, 8, LANES), F32),
        in_specs=[IN_VMEM, ANYWHERE, ANYWHERE, ANYWHERE],
        out_specs=IN_VMEM,
        scratch_shapes=[
            pltpu.VMEM((D, 3 * D), BF16),
            pltpu.VMEM((D, D), BF16),
            pltpu.VMEM((D, E), BF16),
            pltpu.SemaphoreType.DMA((16,)),
        ],
        compiler_params=pltpu.CompilerParams(vmem_limit_bytes=30 << 20),
        cost_estimate=pl.CostEstimate(flops=3 << 30, bytes_accessed=11 << 20, transcendentals=0),
        name="temporal",
    )(
        pltpu.with_memory_space_constraint(x, pltpu.VMEM),
        *(pltpu.with_memory_space_constraint(w, pltpu.HBM) for w in (w_qkv, w_out, w_proj)),
    )


def scale_kernel(*refs):
    out_ref = refs[-1]
    ones = jnp.ones((8, E), BF16)
    rows = refs[0].shape[0]
    for k, ref in enumerate(refs[:-1]):
        squares = ref[...].astype(F32)
        squares = squares * squares
        total = sum(dot_t(ones, part) for part in parts_of(squares, 2))
        out_ref[:, k * rows : (k + 1) * rows] = TEMP / jnp.sqrt(total + EPS)


def caption_scales(pieces):
    return pl.pallas_call(
        scale_kernel,
        out_shape=jax.ShapeDtypeStruct((8, 4 * pieces[0].shape[0]), F32),
        in_specs=[IN_VMEM] * 4,
        out_specs=IN_VMEM,
        compiler_params=pltpu.CompilerParams(vmem_limit_bytes=24 << 20),
        cost_estimate=pl.CostEstimate(flops=20 << 20, bytes_accessed=1 << 20, transcendentals=0),
        name="caption_scales",
    )(*pieces)


def slope(logits, hit):
    sign = jnp.where(hit, 1.0, -1.0)
    return -sign / (1.0 + jnp.exp(sign * logits))


def clip_kernel(parts_ref, *refs):
    pieces, (scale_ref, ids_ref, positive_ref, unit_ref, length_ref, grad_ref) = refs[:4], refs[4:]
    embed = jnp.concatenate(
        [
            jnp.concatenate([parts_ref[2 * c, j : j + 1, :] + parts_ref[2 * c + 1, j : j + 1, :] for j in range(E // LANES)], axis=1)
            for c in range(4)
        ],
        axis=0,
    )
    length = jnp.sqrt(jnp.sum(embed * embed, axis=-1, keepdims=True) + EPS)
    unit = embed / length
    unit_ref[:, :E] = unit
    unit_ref[:, E:] = positive_ref[...]
    length_ref[...] = jnp.broadcast_to(length, length_ref.shape)
    terms = jnp.concatenate(parts_of(unit, 3), axis=0)
    caps = [ref[...] for ref in pieces]
    scale = scale_ref[:1]
    logits = jnp.concatenate([dot_t(terms, cap) for cap in caps], axis=1)
    logits = (logits[:4] + logits[4:8] + logits[8:12]) * scale + BIAS
    weight = slope(logits, ids_ref[...] == positive_ref[:, :1])
    grad = dot(jnp.concatenate(parts_of(weight * scale, 3), axis=0), jnp.concatenate(caps, axis=0))
    grad_ref[...] = grad[:4] + grad[4:8] + grad[8:12]


def clip_part(parts, pieces, scales, ids, positive):
    return pl.pallas_call(
        clip_kernel,
        out_shape=(
            jax.ShapeDtypeStruct((4, E + LANES), F32),
            jax.ShapeDtypeStruct((4, LANES), F32),
            jax.ShapeDtypeStruct((4, E), F32),
        ),
        compiler_params=pltpu.CompilerParams(vmem_limit_bytes=24 << 20),
        cost_estimate=pl.CostEstimate(flops=100 << 20, bytes_accessed=1 << 20, transcendentals=0),
        name="clip_part",
    )(parts, *pieces, scales, ids, positive)


def caption_sum(cap_unit, rows, ids):
    unit = rows[:, :E]
    positive = rows[:, E:].T[:1]
    logits = lax.dot_general(
        cap_unit, unit, (((1,), (1,)), ((), ())), precision=lax.Precision.HIGHEST, preferred_element_type=F32
    )
    weight = slope(TEMP * logits + BIAS, ids[:, : rows.shape[0]] == positive)
    return TEMP * jnp.dot(weight, unit, precision=lax.Precision.HIGHEST, preferred_element_type=F32)


def stacked(ref):
    return jnp.concatenate([ref[g] for g in range(ref.shape[0])], axis=0)


def near_kernel(units_ref, cap_ref, ids_ref, out_ref):
    cap = cap_ref[...].astype(F32)
    length = jnp.sqrt(jnp.sum(cap * cap, axis=-1, keepdims=True) + EPS)
    out_ref[...] = caption_sum(cap / length, stacked(units_ref), ids_ref[...])


def far_kernel(units_ref, part_ref, cap_ref, ids_ref, out_ref):
    cap = cap_ref[...].astype(F32)
    length = jnp.sqrt(jnp.sum(cap * cap, axis=-1, keepdims=True) + EPS)
    cap_unit = cap / length
    grad = part_ref[...] + caption_sum(cap_unit, stacked(units_ref), ids_ref[...])
    out_ref[...] = (grad - cap_unit * jnp.sum(cap_unit * grad, axis=-1, keepdims=True)) / length


def swapped(value, axis, bit):
    return lax.ppermute(value, axis, [(i, i ^ bit) for i in range(lax.axis_size(axis))])


def per_device(video, w_qkv, w_out, w_proj, captions, positive):
    wide = lax.axis_size("wide")
    narrow = lax.axis_size("narrow")
    rank_wide = lax.axis_index("wide")
    rank_narrow = lax.axis_index("narrow")
    cap_rows = captions.shape[0]
    chips = wide // 2
    same_core = [[2 * g + core for g in range(chips)] for core in range(2)]

    send = video.reshape(4, 2, 8, 8, D).transpose(0, 2, 1, 3, 4).reshape(8, 64, D)
    tokens = lax.all_to_all(send, "narrow", 0, 0, tiled=True)

    near = jnp.concatenate([captions, swapped(captions, "wide", 16)], axis=0)
    near = jnp.concatenate([near] + [swapped(near, "wide", bit) for bit in (4, 8, 12)], axis=0)
    source = jnp.stack([rank_wide, rank_wide ^ 16])
    source = jnp.concatenate([source ^ bit for bit in (0, 4, 8, 12)])
    pieces = [near] + [swapped(near, "wide", bit) for bit in (1, 2, 3)]
    source = jnp.concatenate([source ^ bit for bit in range(4)])
    cap_ids = (source[:, None] * narrow + rank_narrow) * cap_rows + jnp.arange(cap_rows, dtype=jnp.int32)[None]
    cap_ids = cap_ids.reshape(1, wide * cap_rows).astype(F32)
    own_ids = (rank_wide * narrow + rank_narrow) * cap_rows + jnp.arange(cap_rows, dtype=jnp.int32)
    own_ids = jnp.broadcast_to(own_ids.astype(F32)[:, None], (cap_rows, LANES))
    positive = jnp.broadcast_to(positive.astype(F32)[:, None], (4, LANES))

    parts = lax.all_to_all(temporal(tokens, w_qkv, w_out, w_proj), "narrow", 0, 0, tiled=True)
    unit, length, grad_unit = clip_part(parts, pieces, caption_scales(pieces), cap_ids, positive)
    outgoing = jnp.broadcast_to(unit[None], (chips, *unit.shape))
    units = lax.all_to_all(outgoing, "wide", 0, 0, axis_index_groups=same_core, tiled=True)
    other = swapped(units, "wide", 1)
    small = pltpu.CompilerParams(vmem_limit_bytes=24 << 20)
    shape = jax.ShapeDtypeStruct(captions.shape, F32)
    part = pl.pallas_call(near_kernel, out_shape=shape, compiler_params=small, name="caption_near")(units, captions, own_ids)
    caption_grad = pl.pallas_call(far_kernel, out_shape=shape, compiler_params=small, name="caption_far")(
        other, part, captions, own_ids
    )
    for bit in (1, 2, 4):
        grad_unit = grad_unit + swapped(grad_unit, "narrow", bit)
    unit = unit[:, :E]
    clip_grad = (grad_unit - unit * jnp.sum(unit * grad_unit, axis=-1, keepdims=True)) / length[:, :1]
    return (clip_grad, caption_grad)


def solution(mesh):
    in_specs = (
        P("wide", "narrow", None, None),
        P(),
        P(),
        P(),
        P(("wide", "narrow"), None),
        P("wide"),
    )
    out_specs = (P("wide", None), P(("wide", "narrow"), None))
    return jax.shard_map(
        per_device, mesh=mesh, in_specs=in_specs, out_specs=out_specs, check_vma=False
    )
```

```python
import functools

import jax
import jax.numpy as jnp
from jax import lax
from jax.experimental import pallas as pl
from jax.experimental.pallas import tpu as pltpu
from jax.sharding import PartitionSpec as P

D = 1024
E = 768
HEADS = 16
HEAD = D // HEADS
FRAMES = 16
SPATIAL = 64
TOKENS = FRAMES * SPATIAL
LANES = 128
GROUP = 4
WIDTH = GROUP * HEAD
BLOCKS = 4
ROWS = FRAMES * 8

TEMP = 10.0
BIAS = -2.0
EPS = 1e-06
LOG2E = 1.4426950408889634

ANYWHERE = pl.BlockSpec(memory_space=pl.ANY)
IN_VMEM = pl.BlockSpec(memory_space=pltpu.VMEM)

F32 = jnp.float32
BF16 = jnp.bfloat16


def dot(a, b):
    return jnp.dot(a, b, preferred_element_type=F32)


def dot_t(a, b):
    return lax.dot_general(a, b, (((1,), (1,)), ((), ())), preferred_element_type=F32)


def parts_of(value, count):
    terms = []
    for _ in range(count):
        term = value.astype(BF16)
        terms.append(term)
        value = value - term.astype(F32)
    return terms


def temporal_kernel(x_ref, wqkv_hbm, wout_hbm, wproj_hbm, out_ref, wqkv, wout, wproj, sems):
    copies = []

    def bring(source, target, columns):
        copy = pltpu.make_async_copy(source.at[:, columns], target.at[:, columns], sems.at[len(copies)])
        copy.start()
        copies.append(copy)

    for start, width in ((0, WIDTH), (WIDTH, WIDTH), (2 * WIDTH, 2 * WIDTH)):
        bring(wqkv_hbm, wqkv, pl.ds(start, width))
        bring(wqkv_hbm, wqkv, pl.ds(D + start, width))
    bring(wqkv_hbm, wqkv, pl.ds(2 * D, D))
    bring(wout_hbm, wout, pl.ds(0, D))
    bring(wproj_hbm, wproj, pl.ds(0, E))

    x = jnp.concatenate([x_ref[:, 16 * b : 16 * b + 16, :].reshape(ROWS, D) for b in range(BLOCKS)], axis=0)
    lane = lax.broadcasted_iota(jnp.int32, (ROWS, WIDTH), 1) // HEAD
    same = lax.broadcasted_iota(jnp.int32, (8, GROUP * ROWS), 0) == lax.broadcasted_iota(jnp.int32, (8, GROUP * ROWS), 1) % 8
    owner = lax.broadcasted_iota(jnp.int32, (GROUP * ROWS, LANES), 0) // ROWS
    column = lax.broadcasted_iota(jnp.int32, (GROUP * ROWS, LANES), 1)
    weights = jnp.zeros((BLOCKS * ROWS, LANES), F32)
    def project(j):
        query = dot(x, wqkv[:, j * WIDTH : (j + 1) * WIDTH]).astype(BF16)
        keys = dot(x, wqkv[:, D + j * WIDTH : D + (j + 1) * WIDTH]).astype(BF16)
        return query, keys

    def attend(query, keys, b):
        q = query[b * ROWS : (b + 1) * ROWS]
        k = keys[b * ROWS : (b + 1) * ROWS]
        split = jnp.concatenate([jnp.where(lane == h, q, jnp.zeros_like(q)) for h in range(GROUP)], axis=0)
        scores = dot_t(k, split).reshape(FRAMES, 8, GROUP * ROWS)
        top = jnp.max(scores, axis=0, keepdims=True)
        expo = jnp.exp2((scores - top) * (HEAD**-0.5 * LOG2E))
        total = jnp.sum(expo, axis=0, keepdims=True)
        return (expo * jnp.where(same, 1.0 / total, 0.0)).astype(BF16).reshape(ROWS, GROUP * ROWS)

    def place(j):
        return jnp.where(owner + j * GROUP == column, 1.0, 0.0).astype(BF16)

    copies[0].wait()
    copies[1].wait()
    ready = project(0)
    for j in range(HEADS // GROUP):
        current = ready
        if j < 2:
            copies[2 * j + 2].wait()
            copies[2 * j + 3].wait()
        if j + 1 < HEADS // GROUP:
            ready = project(j + 1)
        probs = [attend(*current, b) for b in range(BLOCKS)]
        weights += dot(jnp.concatenate(probs, axis=0), place(j))
    left = parts_of(weights.T[:HEADS], 2) + [jnp.ones((HEADS, BLOCKS * ROWS), BF16)]
    sums = dot(jnp.concatenate(left, axis=0), x)
    heads = sums[:HEADS] + sums[HEADS : 2 * HEADS]
    rows = sums[2 * HEADS : 2 * HEADS + 1]
    copies[-3].wait()
    values = dot(jnp.concatenate(parts_of(heads, 2), axis=0), wqkv[:, 2 * D :])
    values = values[:HEADS] + values[HEADS:]
    own = lax.broadcasted_iota(jnp.int32, (HEADS, D), 0) == lax.broadcasted_iota(jnp.int32, (HEADS, D), 1) // HEAD
    mixed = jnp.sum(jnp.where(own, values, 0.0), axis=0, keepdims=True)
    copies[-2].wait()
    mixed = jnp.concatenate([jnp.broadcast_to(part, (8, D)) for part in parts_of(mixed, 2)], axis=0)
    layer = dot(mixed, wout[...])
    pooled = (rows + layer[:1] + layer[8:9]) * (1.0 / TOKENS)
    copies[-1].wait()
    pooled = jnp.concatenate([jnp.broadcast_to(part, (8, D)) for part in parts_of(pooled, 3)], axis=0)
    embed = dot(pooled, wproj[...])
    embed = embed[:8] + embed[8:16] + embed[16:24]
    for j in range(E // LANES):
        out_ref[:, j, :] = embed[:, j * LANES : (j + 1) * LANES]
    out_ref[:, E // LANES :, :] = jnp.zeros((8, 8 - E // LANES, LANES), F32)


def temporal(x, w_qkv, w_out, w_proj):
    return pl.pallas_call(
        temporal_kernel,
        out_shape=pltpu.HBM((8, 8, LANES), F32),
        in_specs=[IN_VMEM, ANYWHERE, ANYWHERE, ANYWHERE],
        out_specs=IN_VMEM,
        scratch_shapes=[
            pltpu.VMEM((D, 3 * D), BF16),
            pltpu.VMEM((D, D), BF16),
            pltpu.VMEM((D, E), BF16),
            pltpu.SemaphoreType.DMA((16,)),
        ],
        compiler_params=pltpu.CompilerParams(vmem_limit_bytes=30 << 20),
        cost_estimate=pl.CostEstimate(flops=3 << 30, bytes_accessed=11 << 20, transcendentals=0),
        name="temporal",
    )(
        pltpu.with_memory_space_constraint(x, pltpu.VMEM),
        *(pltpu.with_memory_space_constraint(w, pltpu.HBM) for w in (w_qkv, w_out, w_proj)),
    )


def slope(logits, hit):
    sign = jnp.where(hit, 1.0, -1.0)
    return -sign / (1.0 + jnp.exp(sign * logits))


def caption_ids(shape, dimension, rows, gathered):
    spot = lax.broadcasted_iota(jnp.int32, shape, dimension)
    block = spot // rows
    source = lax.axis_index("wide") * jnp.ones(shape, jnp.int32)
    if gathered:
        source = source ^ (block // 8) ^ (block // 2 % 4 * 4) ^ (block % 2 * 16)
    return (source * lax.axis_size("narrow") + lax.axis_index("narrow")) * rows + spot % rows


def inverse_lengths(cap):
    ones = jnp.ones((8, E), BF16)
    squares = cap.astype(F32)
    squares = squares * squares
    total = sum(dot_t(ones, part) for part in parts_of(squares, 2))
    return 1.0 / jnp.sqrt(total[:1] + EPS)


def join_kernel(after_ref, *refs):
    rows = refs[0].shape[0]
    for k, ref in enumerate(refs[:-1]):
        refs[-1][k * rows : (k + 1) * rows] = ref[...]


def join(after, arrays):
    rows, columns = arrays[0].shape
    return pl.pallas_call(
        join_kernel,
        out_shape=jax.ShapeDtypeStruct((len(arrays) * rows, columns), arrays[0].dtype),
        in_specs=[ANYWHERE] + [IN_VMEM] * len(arrays),
        out_specs=IN_VMEM,
        compiler_params=pltpu.CompilerParams(vmem_limit_bytes=16 << 20),
        name="join",
    )(pltpu.with_memory_space_constraint(after, pltpu.HBM), *arrays)


def scale_kernel(*refs):
    rows = refs[0].shape[0]
    for k, ref in enumerate(refs[:-1]):
        refs[-1][:, k * rows : (k + 1) * rows] = TEMP * inverse_lengths(ref[...])


def caption_scales(pieces):
    return pl.pallas_call(
        scale_kernel,
        out_shape=jax.ShapeDtypeStruct((1, 4 * pieces[0].shape[0]), F32),
        in_specs=[IN_VMEM] * 4,
        out_specs=IN_VMEM,
        compiler_params=pltpu.CompilerParams(vmem_limit_bytes=24 << 20),
        cost_estimate=pl.CostEstimate(flops=20 << 20, bytes_accessed=1 << 20, transcendentals=0),
        name="caption_scales",
    )(*pieces)


def clip_kernel(rows, positive_ref, parts_ref, scale_ref, *refs):
    pieces, (unit_ref, length_ref, grad_ref, send_ref) = refs[:4], refs[4:]
    embed = jnp.concatenate(
        [
            jnp.concatenate([parts_ref[2 * c, j : j + 1, :] + parts_ref[2 * c + 1, j : j + 1, :] for j in range(E // LANES)], axis=1)
            for c in range(4)
        ],
        axis=0,
    )
    length = jnp.sqrt(jnp.sum(embed * embed, axis=-1, keepdims=True) + EPS)
    unit = embed / length
    clip = lax.broadcasted_iota(jnp.int32, (4, LANES), 0)
    positive = jnp.zeros((4, LANES), jnp.int32)
    for c in range(4):
        positive = jnp.where(clip == c, positive_ref[c], positive)
    unit_ref[:, :E] = unit
    unit_ref[:, E:] = positive.astype(F32)
    length_ref[...] = jnp.broadcast_to(length, length_ref.shape)
    for k in range(send_ref.shape[0]):
        send_ref[k, :, :E] = unit
        send_ref[k, :, E:] = positive.astype(F32)
    terms = jnp.concatenate(parts_of(unit, 3), axis=0)
    caps = [ref[...] for ref in pieces]
    scale = scale_ref[...]
    logits = jnp.concatenate([dot_t(terms, cap) for cap in caps], axis=1)
    logits = (logits[:4] + logits[4:8] + logits[8:12]) * scale + BIAS
    weight = slope(logits, caption_ids(logits.shape, 1, rows, True) == positive[:, :1])
    grad = dot(jnp.concatenate(parts_of(weight * scale, 3), axis=0), jnp.concatenate(caps, axis=0))
    grad_ref[...] = grad[:4] + grad[4:8] + grad[8:12]


def clip_part(positive, parts, scales, pieces, rows, copies):
    return pl.pallas_call(
        functools.partial(clip_kernel, rows),
        out_shape=(
            jax.ShapeDtypeStruct((4, E + LANES), F32),
            jax.ShapeDtypeStruct((4, LANES), F32),
            jax.ShapeDtypeStruct((4, E), F32),
            pltpu.HBM((copies, 4, E + LANES), F32),
        ),
        in_specs=[pl.BlockSpec(memory_space=pltpu.SMEM)] + [IN_VMEM] * 6,
        out_specs=(IN_VMEM,) * 4,
        compiler_params=pltpu.CompilerParams(vmem_limit_bytes=24 << 20),
        cost_estimate=pl.CostEstimate(flops=100 << 20, bytes_accessed=1 << 20, transcendentals=0),
        name="clip_part",
    )(positive, parts, scales, *pieces)


def caption_sum(cap_unit, rows):
    unit = rows[:, :E]
    positive = rows[:, E:].T[:1]
    logits = lax.dot_general(
        cap_unit, unit, (((1,), (1,)), ((), ())), precision=lax.Precision.HIGHEST, preferred_element_type=F32
    )
    ids = caption_ids(logits.shape, 0, logits.shape[0], False).astype(F32)
    weight = slope(TEMP * logits + BIAS, ids == positive)
    return TEMP * jnp.dot(weight, unit, precision=lax.Precision.HIGHEST, preferred_element_type=F32)


def stacked(ref):
    return jnp.concatenate([ref[g] for g in range(ref.shape[0])], axis=0)


def near_kernel(units_ref, cap_ref, out_ref):
    cap = cap_ref[...].astype(F32)
    length = jnp.sqrt(jnp.sum(cap * cap, axis=-1, keepdims=True) + EPS)
    out_ref[...] = caption_sum(cap / length, stacked(units_ref))


def far_kernel(units_ref, part_ref, cap_ref, out_ref):
    cap = cap_ref[...].astype(F32)
    length = jnp.sqrt(jnp.sum(cap * cap, axis=-1, keepdims=True) + EPS)
    cap_unit = cap / length
    grad = part_ref[...] + caption_sum(cap_unit, stacked(units_ref))
    out_ref[...] = (grad - cap_unit * jnp.sum(cap_unit * grad, axis=-1, keepdims=True)) / length


def swapped(value, axis, bit):
    return lax.ppermute(value, axis, [(i, i ^ bit) for i in range(lax.axis_size(axis))])


def per_device(video, w_qkv, w_out, w_proj, captions, positive):
    wide = lax.axis_size("wide")
    chips = wide // 2
    same_core = [[2 * g + core for g in range(chips)] for core in range(2)]

    send = video.reshape(4, 2, 8, 8, D).transpose(0, 2, 1, 3, 4).reshape(8, 64, D)
    tokens = lax.all_to_all(send, "narrow", 0, 0, tiled=True)

    near = jnp.concatenate([captions, swapped(captions, "wide", 16)], axis=0)
    layers = [near] + [swapped(near, "wide", bit) for bit in (4, 8, 12)]

    parts = temporal(tokens, w_qkv, w_out, w_proj)
    near = join(parts, layers)
    pieces = [near] + [swapped(near, "wide", bit) for bit in (1, 2, 3)]
    parts = lax.all_to_all(parts, "narrow", 0, 0, tiled=True)
    unit, length, grad_unit, outgoing = clip_part(
        positive, parts, caption_scales(pieces), pieces, captions.shape[0], chips
    )
    units = lax.all_to_all(outgoing, "wide", 0, 0, axis_index_groups=same_core, tiled=True)
    other = swapped(units, "wide", 1)
    small = pltpu.CompilerParams(vmem_limit_bytes=24 << 20)
    shape = jax.ShapeDtypeStruct(captions.shape, F32)
    part = pl.pallas_call(near_kernel, out_shape=shape, compiler_params=small, name="caption_near")(units, captions)
    caption_grad = pl.pallas_call(far_kernel, out_shape=shape, compiler_params=small, name="caption_far")(other, part, captions)

    others = [swapped(grad_unit, "narrow", bit) for bit in (1, 2, 3)]
    grad_unit = (grad_unit + others[0]) + (others[1] + others[2])
    grad_unit = grad_unit + swapped(grad_unit, "narrow", 4)
    unit = unit[:, :E]
    clip_grad = (grad_unit - unit * jnp.sum(unit * grad_unit, axis=-1, keepdims=True)) / length[:, :1]
    return (clip_grad, caption_grad)


def solution(mesh):
    in_specs = (
        P("wide", "narrow", None, None),
        P(),
        P(),
        P(),
        P(("wide", "narrow"), None),
        P("wide"),
    )
    out_specs = (P("wide", None), P(("wide", "narrow"), None))
    return jax.shard_map(
        per_device, mesh=mesh, in_specs=in_specs, out_specs=out_specs, check_vma=False
    )
```

```python
import functools

import jax
import jax.numpy as jnp
from jax import lax
from jax.experimental import pallas as pl
from jax.experimental.pallas import tpu as pltpu
from jax.sharding import PartitionSpec as P

D = 1024
E = 768
HEADS = 16
HEAD = D // HEADS
FRAMES = 16
SPATIAL = 64
TOKENS = FRAMES * SPATIAL
LANES = 128
GROUP = 4
WIDTH = GROUP * HEAD
BLOCKS = 4
ROWS = FRAMES * 8

TEMP = 10.0
BIAS = -2.0
EPS = 1e-06
LOG2E = 1.4426950408889634

ANYWHERE = pl.BlockSpec(memory_space=pl.ANY)
IN_VMEM = pl.BlockSpec(memory_space=pltpu.VMEM)

F32 = jnp.float32
BF16 = jnp.bfloat16


def dot(a, b):
    return jnp.dot(a, b, preferred_element_type=F32)


def dot_t(a, b):
    return lax.dot_general(a, b, (((1,), (1,)), ((), ())), preferred_element_type=F32)


def parts_of(value, count):
    terms = []
    for _ in range(count):
        term = value.astype(BF16)
        terms.append(term)
        value = value - term.astype(F32)
    return terms


def temporal_kernel(x_ref, wqkv_hbm, wout_hbm, wproj_hbm, out_ref, wqkv, wout, wproj, sems):
    copies = []

    def bring(source, target, columns):
        copy = pltpu.make_async_copy(source.at[:, columns], target.at[:, columns], sems.at[len(copies)])
        copy.start()
        copies.append(copy)

    for start, width in ((0, WIDTH), (WIDTH, WIDTH), (2 * WIDTH, 2 * WIDTH)):
        bring(wqkv_hbm, wqkv, pl.ds(start, width))
        bring(wqkv_hbm, wqkv, pl.ds(D + start, width))
    bring(wqkv_hbm, wqkv, pl.ds(2 * D, D))
    bring(wout_hbm, wout, pl.ds(0, D))
    bring(wproj_hbm, wproj, pl.ds(0, E))

    x = jnp.concatenate([x_ref[:, 16 * b : 16 * b + 16, :].reshape(ROWS, D) for b in range(BLOCKS)], axis=0)
    lane = lax.broadcasted_iota(jnp.int32, (ROWS, WIDTH), 1) // HEAD
    same = lax.broadcasted_iota(jnp.int32, (8, GROUP * ROWS), 0) == lax.broadcasted_iota(jnp.int32, (8, GROUP * ROWS), 1) % 8
    owner = lax.broadcasted_iota(jnp.int32, (GROUP * ROWS, LANES), 0) // ROWS
    column = lax.broadcasted_iota(jnp.int32, (GROUP * ROWS, LANES), 1)
    weights = jnp.zeros((BLOCKS * ROWS, LANES), F32)
    def project(j):
        query = dot(x, wqkv[:, j * WIDTH : (j + 1) * WIDTH]).astype(BF16)
        keys = dot(x, wqkv[:, D + j * WIDTH : D + (j + 1) * WIDTH]).astype(BF16)
        return query, keys

    def attend(query, keys, b):
        q = query[b * ROWS : (b + 1) * ROWS]
        k = keys[b * ROWS : (b + 1) * ROWS]
        split = jnp.concatenate([jnp.where(lane == h, q, jnp.zeros_like(q)) for h in range(GROUP)], axis=0)
        scores = dot_t(k, split).reshape(FRAMES, 8, GROUP * ROWS)
        top = jnp.max(scores, axis=0, keepdims=True)
        expo = jnp.exp2((scores - top) * (HEAD**-0.5 * LOG2E))
        total = jnp.sum(expo, axis=0, keepdims=True)
        return (expo * jnp.where(same, 1.0 / total, 0.0)).astype(BF16).reshape(ROWS, GROUP * ROWS)

    def place(j):
        return jnp.where(owner + j * GROUP == column, 1.0, 0.0).astype(BF16)

    copies[0].wait()
    copies[1].wait()
    ready = project(0)
    for j in range(HEADS // GROUP):
        current = ready
        if j < 2:
            copies[2 * j + 2].wait()
            copies[2 * j + 3].wait()
        if j + 1 < HEADS // GROUP:
            ready = project(j + 1)
        probs = [attend(*current, b) for b in range(BLOCKS)]
        weights += dot(jnp.concatenate(probs, axis=0), place(j))
    left = parts_of(weights.T[:HEADS], 2) + [jnp.ones((HEADS, BLOCKS * ROWS), BF16)]
    sums = dot(jnp.concatenate(left, axis=0), x)
    heads = sums[:HEADS] + sums[HEADS : 2 * HEADS]
    rows = sums[2 * HEADS : 2 * HEADS + 1]
    copies[-3].wait()
    values = dot(jnp.concatenate(parts_of(heads, 2), axis=0), wqkv[:, 2 * D :])
    values = values[:HEADS] + values[HEADS:]
    own = lax.broadcasted_iota(jnp.int32, (HEADS, D), 0) == lax.broadcasted_iota(jnp.int32, (HEADS, D), 1) // HEAD
    mixed = jnp.sum(jnp.where(own, values, 0.0), axis=0, keepdims=True)
    copies[-2].wait()
    mixed = jnp.concatenate([jnp.broadcast_to(part, (8, D)) for part in parts_of(mixed, 2)], axis=0)
    layer = dot(mixed, wout[...])
    pooled = (rows + layer[:1] + layer[8:9]) * (1.0 / TOKENS)
    copies[-1].wait()
    pooled = jnp.concatenate([jnp.broadcast_to(part, (8, D)) for part in parts_of(pooled, 3)], axis=0)
    embed = dot(pooled, wproj[...])
    embed = embed[:8] + embed[8:16] + embed[16:24]
    for j in range(E // LANES):
        out_ref[:, j, :] = embed[:, j * LANES : (j + 1) * LANES]
    out_ref[:, E // LANES :, :] = jnp.zeros((8, 8 - E // LANES, LANES), F32)


def temporal(x, w_qkv, w_out, w_proj):
    return pl.pallas_call(
        temporal_kernel,
        out_shape=pltpu.VMEM((8, 8, LANES), F32),
        in_specs=[IN_VMEM, ANYWHERE, ANYWHERE, ANYWHERE],
        out_specs=IN_VMEM,
        scratch_shapes=[
            pltpu.VMEM((D, 3 * D), BF16),
            pltpu.VMEM((D, D), BF16),
            pltpu.VMEM((D, E), BF16),
            pltpu.SemaphoreType.DMA((16,)),
        ],
        compiler_params=pltpu.CompilerParams(vmem_limit_bytes=30 << 20),
        cost_estimate=pl.CostEstimate(flops=3 << 30, bytes_accessed=11 << 20, transcendentals=0),
        name="temporal",
    )(
        pltpu.with_memory_space_constraint(x, pltpu.VMEM),
        *(pltpu.with_memory_space_constraint(w, pltpu.HBM) for w in (w_qkv, w_out, w_proj)),
    )


def slope(logits, hit):
    sign = jnp.where(hit, 1.0, -1.0)
    return -sign / (1.0 + jnp.exp(sign * logits))


def caption_ids(shape, dimension, rows, gathered):
    spot = lax.broadcasted_iota(jnp.int32, shape, dimension)
    block = spot // rows
    source = lax.axis_index("wide") * jnp.ones(shape, jnp.int32)
    if gathered:
        source = source ^ (block // 8 % 2 * 2) ^ (block // 16) ^ (block // 2 % 4 * 4) ^ (block % 2 * 16)
    return (source * lax.axis_size("narrow") + lax.axis_index("narrow")) * rows + spot % rows


def inverse_lengths(cap):
    ones = jnp.ones((8, E), BF16)
    squares = cap.astype(F32)
    squares = squares * squares
    total = sum(dot_t(ones, part) for part in parts_of(squares, 2))
    return 1.0 / jnp.sqrt(total[:1] + EPS)


def join_kernel(after_ref, *refs):
    rows = refs[0].shape[0]
    for k, ref in enumerate(refs[:-1]):
        refs[-1][k * rows : (k + 1) * rows] = ref[...]


def join(after, arrays):
    rows, columns = arrays[0].shape
    return pl.pallas_call(
        join_kernel,
        out_shape=jax.ShapeDtypeStruct((len(arrays) * rows, columns), arrays[0].dtype),
        in_specs=[ANYWHERE] + [IN_VMEM] * len(arrays),
        out_specs=IN_VMEM,
        compiler_params=pltpu.CompilerParams(vmem_limit_bytes=16 << 20),
        name="join",
    )(after, *arrays)


def unit_kernel(positive_ref, parts_ref, unit_ref, length_ref, send_ref):
    embed = jnp.concatenate(
        [
            jnp.concatenate([parts_ref[2 * c, j : j + 1, :] + parts_ref[2 * c + 1, j : j + 1, :] for j in range(E // LANES)], axis=1)
            for c in range(4)
        ],
        axis=0,
    )
    length = jnp.sqrt(jnp.sum(embed * embed, axis=-1, keepdims=True) + EPS)
    unit = embed / length
    positive = positive_ref[...]
    unit_ref[:, :E] = unit
    unit_ref[:, E:] = positive
    length_ref[...] = jnp.broadcast_to(length, length_ref.shape)
    for k in range(send_ref.shape[0]):
        send_ref[k, :, :E] = unit
        send_ref[k, :, E:] = positive


def make_units(positive, parts, copies):
    return pl.pallas_call(
        unit_kernel,
        out_shape=(
            jax.ShapeDtypeStruct((4, E + LANES), F32),
            jax.ShapeDtypeStruct((4, LANES), F32),
            pltpu.HBM((copies, 4, E + LANES), F32),
        ),
        in_specs=[IN_VMEM, IN_VMEM],
        out_specs=(IN_VMEM,) * 3,
        compiler_params=pltpu.CompilerParams(vmem_limit_bytes=8 << 20),
        name="units",
    )(positive, parts)


def clip_kernel(rows, unit_ref, *refs):
    pieces, grad_ref = refs[:-1], refs[-1]
    terms = jnp.concatenate(parts_of(unit_ref[:, :E], 3), axis=0)
    caps = [ref[...] for ref in pieces]
    scale = TEMP * jnp.concatenate([inverse_lengths(cap) for cap in caps], axis=1)
    logits = jnp.concatenate([dot_t(terms, cap) for cap in caps], axis=1)
    logits = (logits[:4] + logits[4:8] + logits[8:12]) * scale + BIAS
    hit = caption_ids(logits.shape, 1, rows, True).astype(F32) == unit_ref[:, E : E + 1]
    grad = dot(jnp.concatenate(parts_of(slope(logits, hit) * scale, 3), axis=0), jnp.concatenate(caps, axis=0))
    grad_ref[...] = grad[:4] + grad[4:8] + grad[8:12]


def clip_part(unit, pieces, rows):
    return pl.pallas_call(
        functools.partial(clip_kernel, rows),
        out_shape=jax.ShapeDtypeStruct((4, E), F32),
        in_specs=[IN_VMEM] * 4,
        out_specs=IN_VMEM,
        compiler_params=pltpu.CompilerParams(vmem_limit_bytes=24 << 20),
        cost_estimate=pl.CostEstimate(flops=100 << 20, bytes_accessed=1 << 20, transcendentals=0),
        name="clip_part",
    )(unit, *pieces)


def caption_sum(cap_unit, rows):
    unit = rows[:, :E]
    positive = rows[:, E:].T[:1]
    logits = lax.dot_general(
        cap_unit, unit, (((1,), (1,)), ((), ())), precision=lax.Precision.HIGHEST, preferred_element_type=F32
    )
    ids = caption_ids(logits.shape, 0, logits.shape[0], False).astype(F32)
    weight = slope(TEMP * logits + BIAS, ids == positive)
    return TEMP * jnp.dot(weight, unit, precision=lax.Precision.HIGHEST, preferred_element_type=F32)


def stacked(ref):
    return jnp.concatenate([ref[g] for g in range(ref.shape[0])], axis=0)


def near_kernel(units_ref, cap_ref, out_ref):
    cap = cap_ref[...].astype(F32)
    length = jnp.sqrt(jnp.sum(cap * cap, axis=-1, keepdims=True) + EPS)
    out_ref[...] = caption_sum(cap / length, stacked(units_ref))


def far_kernel(units_ref, part_ref, cap_ref, out_ref):
    cap = cap_ref[...].astype(F32)
    length = jnp.sqrt(jnp.sum(cap * cap, axis=-1, keepdims=True) + EPS)
    cap_unit = cap / length
    grad = part_ref[...] + caption_sum(cap_unit, stacked(units_ref))
    out_ref[...] = (grad - cap_unit * jnp.sum(cap_unit * grad, axis=-1, keepdims=True)) / length


def swapped(value, axis, bit):
    return lax.ppermute(value, axis, [(i, i ^ bit) for i in range(lax.axis_size(axis))])


def per_device(video, w_qkv, w_out, w_proj, captions, positive):
    wide = lax.axis_size("wide")
    chips = wide // 2
    same_core = [[2 * g + core for g in range(chips)] for core in range(2)]

    send = video.reshape(4, 2, 8, 8, D).transpose(0, 2, 1, 3, 4).reshape(8, 64, D)
    tokens = lax.all_to_all(send, "narrow", 0, 0, tiled=True)

    near = jnp.concatenate([captions, swapped(captions, "wide", 16)], axis=0)
    layers = [near] + [swapped(near, "wide", bit) for bit in (4, 8, 12)]

    parts = temporal(tokens, w_qkv, w_out, w_proj)
    near = join(parts, layers)
    near = [near, swapped(near, "wide", 2)]
    parts = lax.all_to_all(parts, "narrow", 0, 0, tiled=True)
    pieces = near + [swapped(join(parts, near), "wide", 1)]
    positive = jnp.broadcast_to(positive.astype(F32)[:, None], (4, LANES))
    unit, length, outgoing = make_units(positive, parts, chips)
    grad_unit = clip_part(unit, pieces, captions.shape[0])
    units = lax.all_to_all(outgoing, "wide", 0, 0, axis_index_groups=same_core, tiled=True)
    other = swapped(units, "wide", 1)
    small = pltpu.CompilerParams(vmem_limit_bytes=24 << 20)
    shape = jax.ShapeDtypeStruct(captions.shape, F32)
    part = pl.pallas_call(near_kernel, out_shape=shape, compiler_params=small, name="caption_near")(units, captions)
    caption_grad = pl.pallas_call(far_kernel, out_shape=shape, compiler_params=small, name="caption_far")(other, part, captions)

    others = [swapped(grad_unit, "narrow", bit) for bit in (1, 2, 3)]
    grad_unit = (grad_unit + others[0]) + (others[1] + others[2])
    grad_unit = grad_unit + swapped(grad_unit, "narrow", 4)
    unit = unit[:, :E]
    clip_grad = (grad_unit - unit * jnp.sum(unit * grad_unit, axis=-1, keepdims=True)) / length[:, :1]
    return (clip_grad, caption_grad)


def solution(mesh):
    in_specs = (
        P("wide", "narrow", None, None),
        P(),
        P(),
        P(),
        P(("wide", "narrow"), None),
        P("wide"),
    )
    out_specs = (P("wide", None), P(("wide", "narrow"), None))
    return jax.shard_map(
        per_device, mesh=mesh, in_specs=in_specs, out_specs=out_specs, check_vma=False
    )
```

```python
import functools

import jax
import jax.numpy as jnp
from jax import lax
from jax.experimental import pallas as pl
from jax.experimental.pallas import tpu as pltpu
from jax.sharding import PartitionSpec as P

D = 1024
E = 768
HEADS = 16
HEAD = D // HEADS
FRAMES = 16
SPATIAL = 64
TOKENS = FRAMES * SPATIAL
LANES = 128
GROUP = 4
WIDTH = GROUP * HEAD
AHEAD = 2
BLOCKS = 4
ROWS = FRAMES * 8

TEMP = 10.0
BIAS = -2.0
EPS = 1e-06
LOG2E = 1.4426950408889634

ANYWHERE = pl.BlockSpec(memory_space=pl.ANY)
IN_VMEM = pl.BlockSpec(memory_space=pltpu.VMEM)

F32 = jnp.float32
BF16 = jnp.bfloat16


def dot(a, b):
    return jnp.dot(a, b, preferred_element_type=F32)


def dot_t(a, b):
    return lax.dot_general(a, b, (((1,), (1,)), ((), ())), preferred_element_type=F32)


def parts_of(value, count):
    terms = []
    for _ in range(count):
        term = value.astype(BF16)
        terms.append(term)
        value = value - term.astype(F32)
    return terms


def temporal_kernel(x_ref, query_ref, keys_ref, wqkv_hbm, wout_hbm, wproj_hbm, out_ref, wqkv, wout, wproj, sems):
    copies = []

    def bring(source, target, columns):
        copy = pltpu.make_async_copy(source.at[:, columns], target.at[:, columns], sems.at[len(copies)])
        copy.start()
        copies.append(copy)

    for start, width in ((2 * WIDTH, 2 * WIDTH),):
        bring(wqkv_hbm, wqkv, pl.ds(start, width))
        bring(wqkv_hbm, wqkv, pl.ds(D + start, width))
    bring(wqkv_hbm, wqkv, pl.ds(2 * D, D))
    bring(wout_hbm, wout, pl.ds(0, D))
    bring(wproj_hbm, wproj, pl.ds(0, E))

    x = jnp.concatenate([x_ref[:, 16 * b : 16 * b + 16, :].reshape(ROWS, D) for b in range(BLOCKS)], axis=0)
    lane = lax.broadcasted_iota(jnp.int32, (ROWS, WIDTH), 1) // HEAD
    same = lax.broadcasted_iota(jnp.int32, (8, GROUP * ROWS), 0) == lax.broadcasted_iota(jnp.int32, (8, GROUP * ROWS), 1) % 8
    owner = lax.broadcasted_iota(jnp.int32, (GROUP * ROWS, LANES), 0) // ROWS
    column = lax.broadcasted_iota(jnp.int32, (GROUP * ROWS, LANES), 1)
    weights = jnp.zeros((BLOCKS * ROWS, LANES), F32)

    def project(j):
        columns = slice(j * WIDTH, (j + 1) * WIDTH)
        if j < AHEAD:
            query, keys = query_ref[:, columns], keys_ref[:, columns]
        else:
            if j == AHEAD:
                copies[0].wait()
                copies[1].wait()
            query, keys = wqkv[:, columns], wqkv[:, D + j * WIDTH : D + (j + 1) * WIDTH]
        return dot(x, query).astype(BF16), dot(x, keys).astype(BF16)

    def attend(query, keys, b):
        q = query[b * ROWS : (b + 1) * ROWS]
        k = keys[b * ROWS : (b + 1) * ROWS]
        split = jnp.concatenate([jnp.where(lane == h, q, jnp.zeros_like(q)) for h in range(GROUP)], axis=0)
        scores = dot_t(k, split).reshape(FRAMES, 8, GROUP * ROWS)
        top = jnp.max(scores, axis=0, keepdims=True)
        expo = jnp.exp2((scores - top) * (HEAD**-0.5 * LOG2E))
        total = jnp.sum(expo, axis=0, keepdims=True)
        return (expo * jnp.where(same, 1.0 / total, 0.0)).astype(BF16).reshape(ROWS, GROUP * ROWS)

    def place(j):
        return jnp.where(owner + j * GROUP == column, 1.0, 0.0).astype(BF16)

    ready = project(0)
    for j in range(HEADS // GROUP):
        current = ready
        if j + 1 < HEADS // GROUP:
            ready = project(j + 1)
        probs = [attend(*current, b) for b in range(BLOCKS)]
        weights += dot(jnp.concatenate(probs, axis=0), place(j))
    left = parts_of(weights.T[:HEADS], 2) + [jnp.ones((HEADS, BLOCKS * ROWS), BF16)]
    sums = dot(jnp.concatenate(left, axis=0), x)
    heads = sums[:HEADS] + sums[HEADS : 2 * HEADS]
    rows = sums[2 * HEADS : 2 * HEADS + 1]
    copies[-3].wait()
    values = dot(jnp.concatenate(parts_of(heads, 2), axis=0), wqkv[:, 2 * D :])
    values = values[:HEADS] + values[HEADS:]
    own = lax.broadcasted_iota(jnp.int32, (HEADS, D), 0) == lax.broadcasted_iota(jnp.int32, (HEADS, D), 1) // HEAD
    mixed = jnp.sum(jnp.where(own, values, 0.0), axis=0, keepdims=True)
    copies[-2].wait()
    mixed = jnp.concatenate([jnp.broadcast_to(part, (8, D)) for part in parts_of(mixed, 2)], axis=0)
    layer = dot(mixed, wout[...])
    pooled = (rows + layer[:1] + layer[8:9]) * (1.0 / TOKENS)
    copies[-1].wait()
    pooled = jnp.concatenate([jnp.broadcast_to(part, (8, D)) for part in parts_of(pooled, 3)], axis=0)
    embed = dot(pooled, wproj[...])
    embed = embed[:8] + embed[8:16] + embed[16:24]
    for j in range(E // LANES):
        out_ref[:, j, :] = embed[:, j * LANES : (j + 1) * LANES]
    out_ref[:, E // LANES :, :] = jnp.zeros((8, 8 - E // LANES, LANES), F32)


def fetch_kernel(source, query_ref, keys_ref, sems):
    copies = [
        pltpu.make_async_copy(source.at[:, pl.ds(k * D, AHEAD * WIDTH)], target, sems.at[k])
        for k, target in enumerate((query_ref, keys_ref))
    ]
    for copy in copies:
        copy.start()
    for copy in copies:
        copy.wait()


def fetch(w_qkv):
    return pl.pallas_call(
        fetch_kernel,
        out_shape=(pltpu.VMEM((D, AHEAD * WIDTH), BF16),) * 2,
        in_specs=[ANYWHERE],
        out_specs=(IN_VMEM,) * 2,
        scratch_shapes=[pltpu.SemaphoreType.DMA((2,))],
        compiler_params=pltpu.CompilerParams(vmem_limit_bytes=4 << 20),
        cost_estimate=pl.CostEstimate(flops=0, bytes_accessed=4 << 20, transcendentals=0),
        name="fetch",
    )(pltpu.with_memory_space_constraint(w_qkv, pltpu.HBM))


def temporal(x, first, w_qkv, w_out, w_proj):
    return pl.pallas_call(
        temporal_kernel,
        out_shape=pltpu.VMEM((8, 8, LANES), F32),
        in_specs=[IN_VMEM] * 3 + [ANYWHERE] * 3,
        out_specs=IN_VMEM,
        scratch_shapes=[
            pltpu.VMEM((D, 3 * D), BF16),
            pltpu.VMEM((D, D), BF16),
            pltpu.VMEM((D, E), BF16),
            pltpu.SemaphoreType.DMA((16,)),
        ],
        compiler_params=pltpu.CompilerParams(vmem_limit_bytes=30 << 20),
        cost_estimate=pl.CostEstimate(flops=3 << 30, bytes_accessed=11 << 20, transcendentals=0),
        name="temporal",
    )(
        *(pltpu.with_memory_space_constraint(a, pltpu.VMEM) for a in (x, *first)),
        *(pltpu.with_memory_space_constraint(w, pltpu.HBM) for w in (w_qkv, w_out, w_proj)),
    )


def slope(logits, hit):
    sign = jnp.where(hit, 1.0, -1.0)
    return -sign / (1.0 + jnp.exp(sign * logits))


def caption_ids(shape, dimension, rows, gathered):
    spot = lax.broadcasted_iota(jnp.int32, shape, dimension)
    block = spot // rows
    source = lax.axis_index("wide") * jnp.ones(shape, jnp.int32)
    if gathered:
        source = source ^ (block // 8 % 2 * 2) ^ (block // 16) ^ (block // 2 % 4 * 4) ^ (block % 2 * 16)
    return (source * lax.axis_size("narrow") + lax.axis_index("narrow")) * rows + spot % rows


def inverse_lengths(cap):
    ones = jnp.ones((8, E), BF16)
    squares = cap.astype(F32)
    squares = squares * squares
    total = sum(dot_t(ones, part) for part in parts_of(squares, 2))
    return 1.0 / jnp.sqrt(total[:1] + EPS)


def join_kernel(after_ref, *refs):
    rows = refs[0].shape[0]
    for k, ref in enumerate(refs[:-1]):
        refs[-1][k * rows : (k + 1) * rows] = ref[...]


def join(after, arrays):
    rows, columns = arrays[0].shape
    return pl.pallas_call(
        join_kernel,
        out_shape=jax.ShapeDtypeStruct((len(arrays) * rows, columns), arrays[0].dtype),
        in_specs=[ANYWHERE] + [IN_VMEM] * len(arrays),
        out_specs=IN_VMEM,
        compiler_params=pltpu.CompilerParams(vmem_limit_bytes=16 << 20),
        name="join",
    )(after, *arrays)


def unit_kernel(positive_ref, parts_ref, unit_ref, length_ref, send_ref):
    embed = jnp.concatenate(
        [
            jnp.concatenate([parts_ref[2 * c, j : j + 1, :] + parts_ref[2 * c + 1, j : j + 1, :] for j in range(E // LANES)], axis=1)
            for c in range(4)
        ],
        axis=0,
    )
    length = jnp.sqrt(jnp.sum(embed * embed, axis=-1, keepdims=True) + EPS)
    unit = embed / length
    positive = positive_ref[...]
    unit_ref[:, :E] = unit
    unit_ref[:, E:] = positive
    length_ref[...] = jnp.broadcast_to(length, length_ref.shape)
    for k in range(send_ref.shape[0]):
        send_ref[k, :, :E] = unit
        send_ref[k, :, E:] = positive


def make_units(positive, parts, copies):
    return pl.pallas_call(
        unit_kernel,
        out_shape=(
            jax.ShapeDtypeStruct((4, E + LANES), F32),
            jax.ShapeDtypeStruct((4, LANES), F32),
            pltpu.HBM((copies, 4, E + LANES), F32),
        ),
        in_specs=[IN_VMEM, IN_VMEM],
        out_specs=(IN_VMEM,) * 3,
        compiler_params=pltpu.CompilerParams(vmem_limit_bytes=8 << 20),
        name="units",
    )(positive, parts)


def clip_kernel(rows, unit_ref, *refs):
    pieces, grad_ref = refs[:-1], refs[-1]
    terms = jnp.concatenate(parts_of(unit_ref[:, :E], 3), axis=0)
    caps = [ref[...] for ref in pieces]
    scale = TEMP * jnp.concatenate([inverse_lengths(cap) for cap in caps], axis=1)
    logits = jnp.concatenate([dot_t(terms, cap) for cap in caps], axis=1)
    logits = (logits[:4] + logits[4:8] + logits[8:12]) * scale + BIAS
    hit = caption_ids(logits.shape, 1, rows, True).astype(F32) == unit_ref[:, E : E + 1]
    grad = dot(jnp.concatenate(parts_of(slope(logits, hit) * scale, 3), axis=0), jnp.concatenate(caps, axis=0))
    grad_ref[...] = grad[:4] + grad[4:8] + grad[8:12]


def clip_part(unit, pieces, rows):
    return pl.pallas_call(
        functools.partial(clip_kernel, rows),
        out_shape=jax.ShapeDtypeStruct((4, E), F32),
        in_specs=[IN_VMEM] * 4,
        out_specs=IN_VMEM,
        compiler_params=pltpu.CompilerParams(vmem_limit_bytes=24 << 20),
        cost_estimate=pl.CostEstimate(flops=100 << 20, bytes_accessed=1 << 20, transcendentals=0),
        name="clip_part",
    )(unit, *pieces)


def caption_sum(cap, length, rows):
    count = cap.shape[0]
    units = parts_of(rows[:, :E], 3)
    positive = rows[:, E:].T[:1]
    logits = sum(dot_t(cap, unit) for unit in units) * (TEMP / length) + BIAS
    ids = caption_ids(logits.shape, 0, count, False).astype(F32)
    weight = jnp.concatenate(parts_of(TEMP * slope(logits, ids == positive), 3), axis=0)
    terms = [dot(weight[: (3 - k) * count], unit) for k, unit in enumerate(units)]
    return sum(term[j * count : (j + 1) * count] for k, term in enumerate(terms) for j in range(3 - k))


def stacked(ref):
    return jnp.concatenate([ref[g] for g in range(ref.shape[0])], axis=0)


def lengths(value):
    return jnp.sqrt(jnp.sum(value * value, axis=-1, keepdims=True) + EPS)


def near_kernel(units_ref, cap_ref, out_ref):
    cap = cap_ref[...]
    out_ref[...] = caption_sum(cap, lengths(cap.astype(F32)), stacked(units_ref))


def far_kernel(units_ref, part_ref, cap_ref, out_ref):
    cap = cap_ref[...]
    value = cap.astype(F32)
    length = lengths(value)
    cap_unit = value / length
    grad = part_ref[...] + caption_sum(cap, length, stacked(units_ref))
    out_ref[...] = (grad - cap_unit * jnp.sum(cap_unit * grad, axis=-1, keepdims=True)) / length


def swapped(value, axis, bit):
    return lax.ppermute(value, axis, [(i, i ^ bit) for i in range(lax.axis_size(axis))])


def per_device(video, w_qkv, w_out, w_proj, captions, positive):
    wide = lax.axis_size("wide")
    chips = wide // 2
    same_core = [[2 * g + core for g in range(chips)] for core in range(2)]

    send = video.reshape(4, 2, 8, 8, D).transpose(0, 2, 1, 3, 4).reshape(8, 64, D)
    tokens = lax.all_to_all(send, "narrow", 0, 0, tiled=True)

    near = jnp.concatenate([captions, swapped(captions, "wide", 16)], axis=0)
    layers = [near] + [swapped(near, "wide", bit) for bit in (4, 8, 12)]

    parts = temporal(tokens, fetch(w_qkv), w_qkv, w_out, w_proj)
    near = join(parts, layers)
    near = [near, swapped(near, "wide", 2)]
    parts = lax.all_to_all(parts, "narrow", 0, 0, tiled=True)
    pieces = near + [swapped(join(parts, near), "wide", 1)]
    positive = jnp.broadcast_to(positive.astype(F32)[:, None], (4, LANES))
    unit, length, outgoing = make_units(positive, parts, chips)
    grad_unit = clip_part(unit, pieces, captions.shape[0])
    units = lax.all_to_all(outgoing, "wide", 0, 0, axis_index_groups=same_core, tiled=True)
    other = swapped(units, "wide", 1)
    small = pltpu.CompilerParams(vmem_limit_bytes=24 << 20)
    shape = jax.ShapeDtypeStruct(captions.shape, F32)
    part = pl.pallas_call(near_kernel, out_shape=shape, compiler_params=small, name="caption_near")(units, captions)
    caption_grad = pl.pallas_call(far_kernel, out_shape=shape, compiler_params=small, name="caption_far")(other, part, captions)

    others = [swapped(grad_unit, "narrow", bit) for bit in (1, 2, 3)]
    grad_unit = (grad_unit + others[0]) + (others[1] + others[2])
    grad_unit = grad_unit + swapped(grad_unit, "narrow", 4)
    unit = unit[:, :E]
    clip_grad = (grad_unit - unit * jnp.sum(unit * grad_unit, axis=-1, keepdims=True)) / length[:, :1]
    return (clip_grad, caption_grad)


def solution(mesh):
    in_specs = (
        P("wide", "narrow", None, None),
        P(),
        P(),
        P(),
        P(("wide", "narrow"), None),
        P("wide"),
    )
    out_specs = (P("wide", None), P(("wide", "narrow"), None))
    return jax.shard_map(
        per_device, mesh=mesh, in_specs=in_specs, out_specs=out_specs, check_vma=False
    )
```

```python
import functools

import jax
import jax.numpy as jnp
from jax import lax
from jax.experimental import pallas as pl
from jax.experimental.pallas import tpu as pltpu
from jax.sharding import PartitionSpec as P

D = 1024
E = 768
HEADS = 16
HEAD = D // HEADS
FRAMES = 16
SPATIAL = 64
TOKENS = FRAMES * SPATIAL
LANES = 128
GROUP = 4
WIDTH = GROUP * HEAD
AHEAD = 2
BLOCKS = 4
ROWS = FRAMES * 8

TEMP = 10.0
BIAS = -2.0
EPS = 1e-06
LOG2E = 1.4426950408889634

ANYWHERE = pl.BlockSpec(memory_space=pl.ANY)
IN_VMEM = pl.BlockSpec(memory_space=pltpu.VMEM)

F32 = jnp.float32
BF16 = jnp.bfloat16


def dot(a, b):
    return jnp.dot(a, b, preferred_element_type=F32)


def dot_t(a, b):
    return lax.dot_general(a, b, (((1,), (1,)), ((), ())), preferred_element_type=F32)


def parts_of(value, count):
    terms = []
    for _ in range(count):
        term = value.astype(BF16)
        terms.append(term)
        value = value - term.astype(F32)
    return terms


def temporal_kernel(x_ref, query_ref, keys_ref, wqkv_hbm, wout_hbm, wproj_hbm, out_ref, wqkv, wout, wproj, sems):
    copies = []

    def bring(source, target, columns):
        copy = pltpu.make_async_copy(source.at[:, columns], target.at[:, columns], sems.at[len(copies)])
        copy.start()
        copies.append(copy)

    for start, width in ((2 * WIDTH, 2 * WIDTH),):
        bring(wqkv_hbm, wqkv, pl.ds(start, width))
        bring(wqkv_hbm, wqkv, pl.ds(D + start, width))

    x = jnp.concatenate([x_ref[:, 16 * b : 16 * b + 16, :].reshape(ROWS, D) for b in range(BLOCKS)], axis=0)
    lane = lax.broadcasted_iota(jnp.int32, (ROWS, WIDTH), 1) // HEAD
    same = lax.broadcasted_iota(jnp.int32, (8, GROUP * ROWS), 0) == lax.broadcasted_iota(jnp.int32, (8, GROUP * ROWS), 1) % 8
    owner = lax.broadcasted_iota(jnp.int32, (GROUP * ROWS, LANES), 0) // ROWS
    column = lax.broadcasted_iota(jnp.int32, (GROUP * ROWS, LANES), 1)
    weights = jnp.zeros((BLOCKS * ROWS, LANES), F32)

    def project(j):
        columns = slice(j * WIDTH, (j + 1) * WIDTH)
        if j < AHEAD:
            query, keys = query_ref[:, columns], keys_ref[:, columns]
        else:
            if j == AHEAD:
                copies[0].wait()
                copies[1].wait()
                bring(wqkv_hbm, wqkv, pl.ds(2 * D, D))
                bring(wout_hbm, wout, pl.ds(0, D))
                bring(wproj_hbm, wproj, pl.ds(0, E))
            query, keys = wqkv[:, columns], wqkv[:, D + j * WIDTH : D + (j + 1) * WIDTH]
        return dot(x, query).astype(BF16), dot(x, keys).astype(BF16)

    def attend(query, keys, b):
        q = query[b * ROWS : (b + 1) * ROWS]
        k = keys[b * ROWS : (b + 1) * ROWS]
        split = jnp.concatenate([jnp.where(lane == h, q, jnp.zeros_like(q)) for h in range(GROUP)], axis=0)
        scores = dot_t(k, split).reshape(FRAMES, 8, GROUP * ROWS)
        top = jnp.max(scores, axis=0, keepdims=True)
        expo = jnp.exp2((scores - top) * (HEAD**-0.5 * LOG2E))
        total = jnp.sum(expo, axis=0, keepdims=True)
        return (expo * jnp.where(same, 1.0 / total, 0.0)).astype(BF16).reshape(ROWS, GROUP * ROWS)

    def place(j):
        return jnp.where(owner + j * GROUP == column, 1.0, 0.0).astype(BF16)

    ready = project(0)
    for j in range(HEADS // GROUP):
        current = ready
        if j + 1 < HEADS // GROUP:
            ready = project(j + 1)
        probs = [attend(*current, b) for b in range(BLOCKS)]
        weights += dot(jnp.concatenate(probs, axis=0), place(j))
    left = parts_of(weights.T[:HEADS], 2) + [jnp.ones((HEADS, BLOCKS * ROWS), BF16)]
    sums = dot(jnp.concatenate(left, axis=0), x)
    heads = sums[:HEADS] + sums[HEADS : 2 * HEADS]
    rows = sums[2 * HEADS : 2 * HEADS + 1]
    copies[-3].wait()
    values = dot(jnp.concatenate(parts_of(heads, 2), axis=0), wqkv[:, 2 * D :])
    values = values[:HEADS] + values[HEADS:]
    own = lax.broadcasted_iota(jnp.int32, (HEADS, D), 0) == lax.broadcasted_iota(jnp.int32, (HEADS, D), 1) // HEAD
    mixed = jnp.sum(jnp.where(own, values, 0.0), axis=0, keepdims=True)
    copies[-2].wait()
    mixed = jnp.concatenate([jnp.broadcast_to(part, (8, D)) for part in parts_of(mixed, 2)], axis=0)
    layer = dot(mixed, wout[...])
    pooled = (rows + layer[:1] + layer[8:9]) * (1.0 / TOKENS)
    copies[-1].wait()
    pooled = jnp.concatenate([jnp.broadcast_to(part, (8, D)) for part in parts_of(pooled, 3)], axis=0)
    embed = dot(pooled, wproj[...])
    embed = embed[:8] + embed[8:16] + embed[16:24]
    for j in range(E // LANES):
        out_ref[:, j, :] = embed[:, j * LANES : (j + 1) * LANES]
    out_ref[:, E // LANES :, :] = jnp.zeros((8, 8 - E // LANES, LANES), F32)


def fetch_kernel(source, query_ref, keys_ref, sems):
    copies = [
        pltpu.make_async_copy(source.at[:, pl.ds(k * D, AHEAD * WIDTH)], target, sems.at[k])
        for k, target in enumerate((query_ref, keys_ref))
    ]
    for copy in copies:
        copy.start()
    for copy in copies:
        copy.wait()


def fetch(w_qkv):
    return pl.pallas_call(
        fetch_kernel,
        out_shape=(pltpu.VMEM((D, AHEAD * WIDTH), BF16),) * 2,
        in_specs=[ANYWHERE],
        out_specs=(IN_VMEM,) * 2,
        scratch_shapes=[pltpu.SemaphoreType.DMA((2,))],
        compiler_params=pltpu.CompilerParams(vmem_limit_bytes=4 << 20),
        cost_estimate=pl.CostEstimate(flops=0, bytes_accessed=4 << 20, transcendentals=0),
        name="fetch",
    )(pltpu.with_memory_space_constraint(w_qkv, pltpu.HBM))


def temporal(x, first, w_qkv, w_out, w_proj):
    return pl.pallas_call(
        temporal_kernel,
        out_shape=pltpu.VMEM((8, 8, LANES), F32),
        in_specs=[IN_VMEM] * 3 + [ANYWHERE] * 3,
        out_specs=IN_VMEM,
        scratch_shapes=[
            pltpu.VMEM((D, 3 * D), BF16),
            pltpu.VMEM((D, D), BF16),
            pltpu.VMEM((D, E), BF16),
            pltpu.SemaphoreType.DMA((16,)),
        ],
        compiler_params=pltpu.CompilerParams(vmem_limit_bytes=30 << 20),
        cost_estimate=pl.CostEstimate(flops=3 << 30, bytes_accessed=11 << 20, transcendentals=0),
        name="temporal",
    )(
        *(pltpu.with_memory_space_constraint(a, pltpu.VMEM) for a in (x, *first)),
        *(pltpu.with_memory_space_constraint(w, pltpu.HBM) for w in (w_qkv, w_out, w_proj)),
    )


def slope(logits, hit):
    sign = jnp.where(hit, 1.0, -1.0)
    return -sign / (1.0 + jnp.exp(sign * logits))


def caption_ids(shape, dimension, rows, gathered):
    spot = lax.broadcasted_iota(jnp.int32, shape, dimension)
    block = spot // rows
    source = lax.axis_index("wide") * jnp.ones(shape, jnp.int32)
    if gathered:
        source = source ^ (block // 8 % 2 * 2) ^ (block // 16) ^ (block // 2 % 4 * 4) ^ (block % 2 * 16)
    return (source * lax.axis_size("narrow") + lax.axis_index("narrow")) * rows + spot % rows


def inverse_lengths(cap):
    ones = jnp.ones((8, E), BF16)
    squares = cap.astype(F32)
    squares = squares * squares
    total = sum(dot_t(ones, part) for part in parts_of(squares, 2))
    return 1.0 / jnp.sqrt(total[:1] + EPS)


def join_kernel(after_ref, *refs):
    rows = refs[0].shape[0]
    for k, ref in enumerate(refs[:-1]):
        refs[-1][k * rows : (k + 1) * rows] = ref[...]


def join(after, arrays):
    rows, columns = arrays[0].shape
    return pl.pallas_call(
        join_kernel,
        out_shape=jax.ShapeDtypeStruct((len(arrays) * rows, columns), arrays[0].dtype),
        in_specs=[ANYWHERE] + [IN_VMEM] * len(arrays),
        out_specs=IN_VMEM,
        compiler_params=pltpu.CompilerParams(vmem_limit_bytes=16 << 20),
        name="join",
    )(after, *arrays)


def unit_kernel(positive_ref, parts_ref, unit_ref, length_ref, send_ref):
    embed = jnp.concatenate(
        [
            jnp.concatenate([parts_ref[2 * c, j : j + 1, :] + parts_ref[2 * c + 1, j : j + 1, :] for j in range(E // LANES)], axis=1)
            for c in range(4)
        ],
        axis=0,
    )
    length = jnp.sqrt(jnp.sum(embed * embed, axis=-1, keepdims=True) + EPS)
    unit = embed / length
    positive = positive_ref[...]
    unit_ref[:, :E] = unit
    unit_ref[:, E:] = positive
    length_ref[...] = jnp.broadcast_to(length, length_ref.shape)
    for k in range(send_ref.shape[0]):
        send_ref[k, :, :E] = unit
        send_ref[k, :, E:] = positive


def make_units(positive, parts, copies):
    return pl.pallas_call(
        unit_kernel,
        out_shape=(
            jax.ShapeDtypeStruct((4, E + LANES), F32),
            jax.ShapeDtypeStruct((4, LANES), F32),
            pltpu.HBM((copies, 4, E + LANES), F32),
        ),
        in_specs=[IN_VMEM, IN_VMEM],
        out_specs=(IN_VMEM,) * 3,
        compiler_params=pltpu.CompilerParams(vmem_limit_bytes=8 << 20),
        name="units",
    )(positive, parts)


def clip_kernel(rows, unit_ref, *refs):
    pieces, grad_ref = refs[:-1], refs[-1]
    terms = jnp.concatenate(parts_of(unit_ref[:, :E], 3), axis=0)
    caps = [ref[...] for ref in pieces]
    scale = TEMP * jnp.concatenate([inverse_lengths(cap) for cap in caps], axis=1)
    logits = jnp.concatenate([dot_t(terms, cap) for cap in caps], axis=1)
    logits = (logits[:4] + logits[4:8] + logits[8:12]) * scale + BIAS
    hit = caption_ids(logits.shape, 1, rows, True).astype(F32) == unit_ref[:, E : E + 1]
    grad = dot(jnp.concatenate(parts_of(slope(logits, hit) * scale, 3), axis=0), jnp.concatenate(caps, axis=0))
    grad_ref[...] = grad[:4] + grad[4:8] + grad[8:12]


def clip_part(unit, pieces, rows):
    return pl.pallas_call(
        functools.partial(clip_kernel, rows),
        out_shape=jax.ShapeDtypeStruct((4, E), F32),
        in_specs=[IN_VMEM] * 4,
        out_specs=IN_VMEM,
        compiler_params=pltpu.CompilerParams(vmem_limit_bytes=24 << 20),
        cost_estimate=pl.CostEstimate(flops=100 << 20, bytes_accessed=1 << 20, transcendentals=0),
        name="clip_part",
    )(unit, *pieces)


def caption_sum(cap, length, rows):
    count = cap.shape[0]
    units = parts_of(rows[:, :E], 3)
    positive = rows[:, E:].T[:1]
    logits = sum(dot_t(cap, unit) for unit in units) * (TEMP / length) + BIAS
    ids = caption_ids(logits.shape, 0, count, False).astype(F32)
    weight = jnp.concatenate(parts_of(TEMP * slope(logits, ids == positive), 3), axis=0)
    terms = [dot(weight[: (3 - k) * count], unit) for k, unit in enumerate(units)]
    return sum(term[j * count : (j + 1) * count] for k, term in enumerate(terms) for j in range(3 - k))


def stacked(ref):
    return jnp.concatenate([ref[g] for g in range(ref.shape[0])], axis=0)


def lengths(value):
    return jnp.sqrt(jnp.sum(value * value, axis=-1, keepdims=True) + EPS)


def near_kernel(units_ref, cap_ref, out_ref):
    cap = cap_ref[...]
    out_ref[...] = caption_sum(cap, lengths(cap.astype(F32)), stacked(units_ref))


def far_kernel(units_ref, part_ref, cap_ref, out_ref):
    cap = cap_ref[...]
    value = cap.astype(F32)
    length = lengths(value)
    cap_unit = value / length
    grad = part_ref[...] + caption_sum(cap, length, stacked(units_ref))
    out_ref[...] = (grad - cap_unit * jnp.sum(cap_unit * grad, axis=-1, keepdims=True)) / length


def swapped(value, axis, bit):
    return lax.ppermute(value, axis, [(i, i ^ bit) for i in range(lax.axis_size(axis))])


def per_device(video, w_qkv, w_out, w_proj, captions, positive):
    wide = lax.axis_size("wide")
    chips = wide // 2
    same_core = [[2 * g + core for g in range(chips)] for core in range(2)]

    send = video.reshape(4, 2, 8, 8, D).transpose(0, 2, 1, 3, 4).reshape(8, 64, D)
    tokens = lax.all_to_all(send, "narrow", 0, 0, tiled=True)

    near = jnp.concatenate([captions, swapped(captions, "wide", 16)], axis=0)
    layers = [near] + [swapped(near, "wide", bit) for bit in (4, 8, 12)]

    parts = temporal(tokens, fetch(w_qkv), w_qkv, w_out, w_proj)
    near = join(parts, layers)
    near = [near, swapped(near, "wide", 2)]
    parts = lax.all_to_all(parts, "narrow", 0, 0, tiled=True)
    pieces = near + [swapped(join(parts, near), "wide", 1)]
    positive = jnp.broadcast_to(positive.astype(F32)[:, None], (4, LANES))
    unit, length, outgoing = make_units(positive, parts, chips)
    grad_unit = clip_part(unit, pieces, captions.shape[0])
    units = lax.all_to_all(outgoing, "wide", 0, 0, axis_index_groups=same_core, tiled=True)
    other = swapped(units, "wide", 1)
    small = pltpu.CompilerParams(vmem_limit_bytes=24 << 20)
    shape = jax.ShapeDtypeStruct(captions.shape, F32)
    part = pl.pallas_call(near_kernel, out_shape=shape, compiler_params=small, name="caption_near")(units, captions)
    caption_grad = pl.pallas_call(far_kernel, out_shape=shape, compiler_params=small, name="caption_far")(other, part, captions)

    others = [swapped(grad_unit, "narrow", bit) for bit in (1, 2, 3)]
    grad_unit = (grad_unit + others[0]) + (others[1] + others[2])
    grad_unit = grad_unit + swapped(grad_unit, "narrow", 4)
    unit = unit[:, :E]
    clip_grad = (grad_unit - unit * jnp.sum(unit * grad_unit, axis=-1, keepdims=True)) / length[:, :1]
    return (clip_grad, caption_grad)


def solution(mesh):
    in_specs = (
        P("wide", "narrow", None, None),
        P(),
        P(),
        P(),
        P(("wide", "narrow"), None),
        P("wide"),
    )
    out_specs = (P("wide", None), P(("wide", "narrow"), None))
    return jax.shard_map(
        per_device, mesh=mesh, in_specs=in_specs, out_specs=out_specs, check_vma=False
    )
```

```python
import functools

import jax
import jax.numpy as jnp
from jax import lax
from jax.experimental import pallas as pl
from jax.experimental.pallas import tpu as pltpu
from jax.sharding import PartitionSpec as P

D = 1024
E = 768
HEADS = 16
HEAD = D // HEADS
FRAMES = 16
SPATIAL = 64
TOKENS = FRAMES * SPATIAL
LANES = 128
GROUP = 4
WIDTH = GROUP * HEAD
AHEAD = 2
BLOCKS = 4
ROWS = FRAMES * 8

TEMP = 10.0
BIAS = -2.0
EPS = 1e-06
LOG2E = 1.4426950408889634

ANYWHERE = pl.BlockSpec(memory_space=pl.ANY)
IN_VMEM = pl.BlockSpec(memory_space=pltpu.VMEM)

F32 = jnp.float32
BF16 = jnp.bfloat16


def dot(a, b):
    return jnp.dot(a, b, preferred_element_type=F32)


def dot_t(a, b):
    return lax.dot_general(a, b, (((1,), (1,)), ((), ())), preferred_element_type=F32)


def parts_of(value, count):
    terms = []
    for _ in range(count):
        term = value.astype(BF16)
        terms.append(term)
        value = value - term.astype(F32)
    return terms


def temporal_kernel(x_ref, query_ref, keys_ref, wqkv_hbm, wout_hbm, wproj_hbm, out_ref, wqkv, wout, wproj, sems):
    copies = []

    def bring(source, target, columns):
        copy = pltpu.make_async_copy(source.at[:, columns], target.at[:, columns], sems.at[len(copies)])
        copy.start()
        copies.append(copy)

    for start, width in ((2 * WIDTH, 2 * WIDTH),):
        bring(wqkv_hbm, wqkv, pl.ds(start, width))
        bring(wqkv_hbm, wqkv, pl.ds(D + start, width))

    x = jnp.concatenate([x_ref[:, 16 * b : 16 * b + 16, :].reshape(ROWS, D) for b in range(BLOCKS)], axis=0)
    lane = lax.broadcasted_iota(jnp.int32, (ROWS, WIDTH), 1) // HEAD
    same = lax.broadcasted_iota(jnp.int32, (8, GROUP * ROWS), 0) == lax.broadcasted_iota(jnp.int32, (8, GROUP * ROWS), 1) % 8
    owner = lax.broadcasted_iota(jnp.int32, (GROUP * ROWS, LANES), 0) // ROWS
    column = lax.broadcasted_iota(jnp.int32, (GROUP * ROWS, LANES), 1)
    weights = jnp.zeros((BLOCKS * ROWS, LANES), F32)

    def project(j):
        columns = slice(j * WIDTH, (j + 1) * WIDTH)
        if j < AHEAD:
            query, keys = query_ref[:, columns], keys_ref[:, columns]
        else:
            if j == AHEAD:
                copies[0].wait()
                copies[1].wait()
                bring(wqkv_hbm, wqkv, pl.ds(2 * D, D))
                bring(wout_hbm, wout, pl.ds(0, D))
                bring(wproj_hbm, wproj, pl.ds(0, E))
            query, keys = wqkv[:, columns], wqkv[:, D + j * WIDTH : D + (j + 1) * WIDTH]
        return dot(x, query).astype(BF16), dot(x, keys).astype(BF16)

    def attend(query, keys, b):
        q = query[b * ROWS : (b + 1) * ROWS]
        k = keys[b * ROWS : (b + 1) * ROWS]
        split = jnp.concatenate([jnp.where(lane == h, q, jnp.zeros_like(q)) for h in range(GROUP)], axis=0)
        scores = dot_t(k, split).reshape(FRAMES, 8, GROUP * ROWS)
        top = jnp.max(scores, axis=0, keepdims=True)
        expo = jnp.exp2((scores - top) * (HEAD**-0.5 * LOG2E))
        total = jnp.sum(expo, axis=0, keepdims=True)
        return (expo * jnp.where(same, 1.0 / total, 0.0)).astype(BF16).reshape(ROWS, GROUP * ROWS)

    def place(j):
        return jnp.where(owner + j * GROUP == column, 1.0, 0.0).astype(BF16)

    ready = project(0)
    for j in range(HEADS // GROUP):
        current = ready
        if j + 1 < HEADS // GROUP:
            ready = project(j + 1)
        probs = [attend(*current, b) for b in range(BLOCKS)]
        weights += dot(jnp.concatenate(probs, axis=0), place(j))
    left = parts_of(weights.T[:HEADS], 2) + [jnp.ones((HEADS, BLOCKS * ROWS), BF16)]
    sums = dot(jnp.concatenate(left, axis=0), x)
    heads = sums[:HEADS] + sums[HEADS : 2 * HEADS]
    rows = sums[2 * HEADS : 2 * HEADS + 1]
    copies[-3].wait()
    values = dot(jnp.concatenate(parts_of(heads, 2), axis=0), wqkv[:, 2 * D :])
    values = values[:HEADS] + values[HEADS:]
    own = lax.broadcasted_iota(jnp.int32, (HEADS, D), 0) == lax.broadcasted_iota(jnp.int32, (HEADS, D), 1) // HEAD
    mixed = jnp.sum(jnp.where(own, values, 0.0), axis=0, keepdims=True)
    copies[-2].wait()
    mixed = jnp.concatenate([jnp.broadcast_to(part, (8, D)) for part in parts_of(mixed, 2)], axis=0)
    layer = dot(mixed, wout[...])
    pooled = (rows + layer[:1] + layer[8:9]) * (1.0 / TOKENS)
    copies[-1].wait()
    pooled = jnp.concatenate([jnp.broadcast_to(part, (8, D)) for part in parts_of(pooled, 3)], axis=0)
    embed = dot(pooled, wproj[...])
    embed = embed[:8] + embed[8:16] + embed[16:24]
    for j in range(E // LANES):
        out_ref[:, j, :] = embed[:, j * LANES : (j + 1) * LANES]
    out_ref[:, E // LANES :, :] = jnp.zeros((8, 8 - E // LANES, LANES), F32)


def fetch_kernel(source, query_ref, keys_ref, sems):
    copies = [
        pltpu.make_async_copy(source.at[:, pl.ds(k * D, AHEAD * WIDTH)], target, sems.at[k])
        for k, target in enumerate((query_ref, keys_ref))
    ]
    for copy in copies:
        copy.start()
    for copy in copies:
        copy.wait()


def fetch(w_qkv):
    return pl.pallas_call(
        fetch_kernel,
        out_shape=(pltpu.VMEM((D, AHEAD * WIDTH), BF16),) * 2,
        in_specs=[ANYWHERE],
        out_specs=(IN_VMEM,) * 2,
        scratch_shapes=[pltpu.SemaphoreType.DMA((2,))],
        compiler_params=pltpu.CompilerParams(vmem_limit_bytes=4 << 20),
        cost_estimate=pl.CostEstimate(flops=0, bytes_accessed=4 << 20, transcendentals=0),
        name="fetch",
    )(pltpu.with_memory_space_constraint(w_qkv, pltpu.HBM))


def temporal(x, first, w_qkv, w_out, w_proj):
    return pl.pallas_call(
        temporal_kernel,
        out_shape=pltpu.VMEM((8, 8, LANES), F32),
        in_specs=[IN_VMEM] * 3 + [ANYWHERE] * 3,
        out_specs=IN_VMEM,
        scratch_shapes=[
            pltpu.VMEM((D, 3 * D), BF16),
            pltpu.VMEM((D, D), BF16),
            pltpu.VMEM((D, E), BF16),
            pltpu.SemaphoreType.DMA((16,)),
        ],
        compiler_params=pltpu.CompilerParams(vmem_limit_bytes=30 << 20),
        cost_estimate=pl.CostEstimate(flops=3 << 30, bytes_accessed=11 << 20, transcendentals=0),
        name="temporal",
    )(
        *(pltpu.with_memory_space_constraint(a, pltpu.VMEM) for a in (x, *first)),
        *(pltpu.with_memory_space_constraint(w, pltpu.HBM) for w in (w_qkv, w_out, w_proj)),
    )


def slope(logits, hit):
    sign = jnp.where(hit, 1.0, -1.0)
    return -sign / (1.0 + jnp.exp(sign * logits))


def caption_ids(shape, dimension, rows, gathered):
    spot = lax.broadcasted_iota(jnp.int32, shape, dimension)
    block = spot // rows
    source = lax.axis_index("wide") * jnp.ones(shape, jnp.int32)
    if gathered:
        source = source ^ (block // 8 % 2 * 2) ^ (block // 16) ^ (block // 2 % 4 * 4) ^ (block % 2 * 16)
    return (source * lax.axis_size("narrow") + lax.axis_index("narrow")) * rows + spot % rows


def inverse_lengths(cap):
    ones = jnp.ones((8, E), BF16)
    squares = cap.astype(F32)
    squares = squares * squares
    total = sum(dot_t(ones, part) for part in parts_of(squares, 2))
    return 1.0 / jnp.sqrt(total[:1] + EPS)


def join_kernel(after_ref, *refs):
    rows = refs[0].shape[0]
    for k, ref in enumerate(refs[:-1]):
        refs[-1][k * rows : (k + 1) * rows] = ref[...]


def join(after, arrays):
    rows, columns = arrays[0].shape
    return pl.pallas_call(
        join_kernel,
        out_shape=jax.ShapeDtypeStruct((len(arrays) * rows, columns), arrays[0].dtype),
        in_specs=[ANYWHERE] + [IN_VMEM] * len(arrays),
        out_specs=IN_VMEM,
        compiler_params=pltpu.CompilerParams(vmem_limit_bytes=16 << 20),
        name="join",
    )(after, *arrays)


def unit_kernel(positive_ref, parts_ref, unit_ref, length_ref, send_ref):
    embed = jnp.concatenate(
        [
            jnp.concatenate([parts_ref[2 * c, j : j + 1, :] + parts_ref[2 * c + 1, j : j + 1, :] for j in range(E // LANES)], axis=1)
            for c in range(4)
        ],
        axis=0,
    )
    length = jnp.sqrt(jnp.sum(embed * embed, axis=-1, keepdims=True) + EPS)
    unit = embed / length
    positive = positive_ref[...]
    unit_ref[:, :E] = unit
    unit_ref[:, E:] = positive
    length_ref[...] = jnp.broadcast_to(length, length_ref.shape)
    for k in range(send_ref.shape[0]):
        send_ref[k, :, :E] = unit
        send_ref[k, :, E:] = positive


def make_units(positive, parts, copies):
    return pl.pallas_call(
        unit_kernel,
        out_shape=(
            jax.ShapeDtypeStruct((4, E + LANES), F32),
            jax.ShapeDtypeStruct((4, LANES), F32),
            pltpu.HBM((copies, 4, E + LANES), F32),
        ),
        in_specs=[IN_VMEM, IN_VMEM],
        out_specs=(IN_VMEM,) * 3,
        compiler_params=pltpu.CompilerParams(vmem_limit_bytes=8 << 20),
        name="units",
    )(positive, parts)


def clip_kernel(rows, unit_ref, *refs):
    pieces, grad_ref = refs[:-1], refs[-1]
    terms = jnp.concatenate(parts_of(unit_ref[:, :E], 3), axis=0)
    caps = [ref[...] for ref in pieces]
    scale = TEMP * jnp.concatenate([inverse_lengths(cap) for cap in caps], axis=1)
    logits = jnp.concatenate([dot_t(terms, cap) for cap in caps], axis=1)
    logits = (logits[:4] + logits[4:8] + logits[8:12]) * scale + BIAS
    hit = caption_ids(logits.shape, 1, rows, True).astype(F32) == unit_ref[:, E : E + 1]
    grad = dot(jnp.concatenate(parts_of(slope(logits, hit) * scale, 3), axis=0), jnp.concatenate(caps, axis=0))
    grad_ref[...] = grad[:4] + grad[4:8] + grad[8:12]


def clip_part(unit, pieces, rows):
    return pl.pallas_call(
        functools.partial(clip_kernel, rows),
        out_shape=jax.ShapeDtypeStruct((4, E), F32),
        in_specs=[IN_VMEM] * 4,
        out_specs=IN_VMEM,
        compiler_params=pltpu.CompilerParams(vmem_limit_bytes=24 << 20),
        cost_estimate=pl.CostEstimate(flops=100 << 20, bytes_accessed=1 << 20, transcendentals=0),
        name="clip_part",
    )(unit, *pieces)


def caption_sum(cap, length, rows):
    count = cap.shape[0]
    units = parts_of(rows[:, :E], 3)
    positive = rows[:, E:].T[:1]
    logits = sum(dot_t(cap, unit) for unit in units) * (TEMP / length) + BIAS
    ids = caption_ids(logits.shape, 0, count, False).astype(F32)
    weight = jnp.concatenate(parts_of(TEMP * slope(logits, ids == positive), 3), axis=0)
    terms = [dot(weight[: (3 - k) * count], unit) for k, unit in enumerate(units)]
    return sum(term[j * count : (j + 1) * count] for k, term in enumerate(terms) for j in range(3 - k))


def stacked(ref):
    return jnp.concatenate([ref[g] for g in range(ref.shape[0])], axis=0)


def lengths(value):
    return jnp.sqrt(jnp.sum(value * value, axis=-1, keepdims=True) + EPS)


def near_kernel(units_ref, cap_ref, out_ref):
    cap = cap_ref[...]
    out_ref[...] = caption_sum(cap, lengths(cap.astype(F32)), stacked(units_ref))


def last_kernel(units_ref, part_ref, cap_ref, own_ref, along_ref, unit_ref, length_ref, caption_ref, clip_ref):
    unit = unit_ref[:, :E]
    grad = own_ref[...]
    clip_ref[...] = (grad - unit * along_ref[...]) / length_ref[:, :1]
    cap = cap_ref[...]
    value = cap.astype(F32)
    length = lengths(value)
    cap_unit = value / length
    grad = part_ref[...] + caption_sum(cap, length, stacked(units_ref))
    caption_ref[...] = (grad - cap_unit * jnp.sum(cap_unit * grad, axis=-1, keepdims=True)) / length


def swapped(value, axis, bit):
    return lax.ppermute(value, axis, [(i, i ^ bit) for i in range(lax.axis_size(axis))])


def per_device(video, w_qkv, w_out, w_proj, captions, positive):
    wide = lax.axis_size("wide")
    chips = wide // 2
    same_core = [[2 * g + core for g in range(chips)] for core in range(2)]

    send = video.reshape(4, 2, 8, 8, D).transpose(0, 2, 1, 3, 4).reshape(8, 64, D)
    tokens = lax.all_to_all(send, "narrow", 0, 0, tiled=True)

    near = jnp.concatenate([captions, swapped(captions, "wide", 16)], axis=0)
    layers = [near] + [swapped(near, "wide", bit) for bit in (4, 8, 12)]

    parts = temporal(tokens, fetch(w_qkv), w_qkv, w_out, w_proj)
    near = join(parts, layers)
    near = [near, swapped(near, "wide", 2)]
    parts = lax.all_to_all(parts, "narrow", 0, 0, tiled=True)
    pieces = near + [swapped(join(parts, near), "wide", 1)]
    positive = jnp.broadcast_to(positive.astype(F32)[:, None], (4, LANES))
    unit, length, outgoing = make_units(positive, parts, chips)
    grad_unit = clip_part(unit, pieces, captions.shape[0])
    units = lax.all_to_all(outgoing, "wide", 0, 0, axis_index_groups=same_core, tiled=True)
    other = swapped(units, "wide", 1)
    small = pltpu.CompilerParams(vmem_limit_bytes=24 << 20)
    shape = jax.ShapeDtypeStruct(captions.shape, F32)
    part = pl.pallas_call(near_kernel, out_shape=shape, compiler_params=small, name="caption_near")(units, captions)
    others = [swapped(grad_unit, "narrow", bit) for bit in (1, 2, 3)]
    grad_unit = (grad_unit + others[0]) + (others[1] + others[2])
    grad_unit = grad_unit + swapped(grad_unit, "narrow", 4)
    along = jnp.sum(unit[:, :E] * grad_unit, axis=-1, keepdims=True)
    caption_grad, clip_grad = pl.pallas_call(
        last_kernel,
        out_shape=(shape, jax.ShapeDtypeStruct((4, E), F32)),
        compiler_params=small,
        name="gradients",
    )(other, part, captions, grad_unit, along, unit, length)
    return (clip_grad, caption_grad)


def solution(mesh):
    in_specs = (
        P("wide", "narrow", None, None),
        P(),
        P(),
        P(),
        P(("wide", "narrow"), None),
        P("wide"),
    )
    out_specs = (P("wide", None), P(("wide", "narrow"), None))
    return jax.shard_map(
        per_device, mesh=mesh, in_specs=in_specs, out_specs=out_specs, check_vma=False
    )
```

```python
import functools

import jax
import jax.numpy as jnp
from jax import lax
from jax.experimental import pallas as pl
from jax.experimental.pallas import tpu as pltpu
from jax.sharding import PartitionSpec as P

D = 1024
E = 768
HEADS = 16
HEAD = D // HEADS
FRAMES = 16
SPATIAL = 64
TOKENS = FRAMES * SPATIAL
LANES = 128
GROUP = 4
WIDTH = GROUP * HEAD
AHEAD = 2
BLOCKS = 4
ROWS = FRAMES * 8

TEMP = 10.0
BIAS = -2.0
EPS = 1e-06
LOG2E = 1.4426950408889634

ANYWHERE = pl.BlockSpec(memory_space=pl.ANY)
IN_VMEM = pl.BlockSpec(memory_space=pltpu.VMEM)

F32 = jnp.float32
BF16 = jnp.bfloat16


def dot(a, b):
    return jnp.dot(a, b, preferred_element_type=F32)


def dot_t(a, b):
    return lax.dot_general(a, b, (((1,), (1,)), ((), ())), preferred_element_type=F32)


def parts_of(value, count):
    terms = []
    for _ in range(count):
        term = value.astype(BF16)
        terms.append(term)
        value = value - term.astype(F32)
    return terms


def temporal_kernel(x_ref, query_ref, keys_ref, wqkv_hbm, wout_hbm, wproj_hbm, out_ref, wqkv, wout, wproj, sems):
    copies = []

    def bring(source, target, columns):
        copy = pltpu.make_async_copy(source.at[:, columns], target.at[:, columns], sems.at[len(copies)])
        copy.start()
        copies.append(copy)

    for start, width in ((2 * WIDTH, 2 * WIDTH),):
        bring(wqkv_hbm, wqkv, pl.ds(start, width))
        bring(wqkv_hbm, wqkv, pl.ds(D + start, width))

    x = jnp.concatenate([x_ref[:, 16 * b : 16 * b + 16, :].reshape(ROWS, D) for b in range(BLOCKS)], axis=0)
    lane = lax.broadcasted_iota(jnp.int32, (ROWS, WIDTH), 1) // HEAD
    same = lax.broadcasted_iota(jnp.int32, (8, GROUP * ROWS), 0) == lax.broadcasted_iota(jnp.int32, (8, GROUP * ROWS), 1) % 8
    owner = lax.broadcasted_iota(jnp.int32, (GROUP * ROWS, LANES), 0) // ROWS
    column = lax.broadcasted_iota(jnp.int32, (GROUP * ROWS, LANES), 1)
    weights = jnp.zeros((BLOCKS * ROWS, LANES), F32)

    def project(j):
        columns = slice(j * WIDTH, (j + 1) * WIDTH)
        if j < AHEAD:
            query, keys = query_ref[:, columns], keys_ref[:, columns]
        else:
            if j == AHEAD:
                copies[0].wait()
                copies[1].wait()
                bring(wqkv_hbm, wqkv, pl.ds(2 * D, D))
                bring(wout_hbm, wout, pl.ds(0, D))
                bring(wproj_hbm, wproj, pl.ds(0, E))
            query, keys = wqkv[:, columns], wqkv[:, D + j * WIDTH : D + (j + 1) * WIDTH]
        return dot(x, query).astype(BF16), dot(x, keys).astype(BF16)

    def attend(query, keys, b):
        q = query[b * ROWS : (b + 1) * ROWS]
        k = keys[b * ROWS : (b + 1) * ROWS]
        split = jnp.concatenate([jnp.where(lane == h, q, jnp.zeros_like(q)) for h in range(GROUP)], axis=0)
        scores = dot_t(k, split).reshape(FRAMES, 8, GROUP * ROWS)
        top = jnp.max(scores, axis=0, keepdims=True)
        expo = jnp.exp2((scores - top) * (HEAD**-0.5 * LOG2E))
        total = jnp.sum(expo, axis=0, keepdims=True)
        return (expo * jnp.where(same, 1.0 / total, 0.0)).astype(BF16).reshape(ROWS, GROUP * ROWS)

    def place(j):
        return jnp.where(owner + j * GROUP == column, 1.0, 0.0).astype(BF16)

    ready = project(0)
    for j in range(HEADS // GROUP):
        current = ready
        if j + 1 < HEADS // GROUP:
            ready = project(j + 1)
        probs = [attend(*current, b) for b in range(BLOCKS)]
        weights += dot(jnp.concatenate(probs, axis=0), place(j))
    left = parts_of(weights.T[:HEADS], 2) + [jnp.ones((HEADS, BLOCKS * ROWS), BF16)]
    sums = dot(jnp.concatenate(left, axis=0), x)
    heads = sums[:HEADS] + sums[HEADS : 2 * HEADS]
    rows = sums[2 * HEADS : 2 * HEADS + 1]
    copies[-3].wait()
    values = dot(jnp.concatenate(parts_of(heads, 2), axis=0), wqkv[:, 2 * D :])
    values = values[:HEADS] + values[HEADS:]
    own = lax.broadcasted_iota(jnp.int32, (HEADS, D), 0) == lax.broadcasted_iota(jnp.int32, (HEADS, D), 1) // HEAD
    mixed = jnp.sum(jnp.where(own, values, 0.0), axis=0, keepdims=True)
    copies[-2].wait()
    mixed = jnp.concatenate([jnp.broadcast_to(part, (8, D)) for part in parts_of(mixed, 2)], axis=0)
    layer = dot(mixed, wout[...])
    pooled = (rows + layer[:1] + layer[8:9]) * (1.0 / TOKENS)
    copies[-1].wait()
    pooled = jnp.concatenate([jnp.broadcast_to(part, (8, D)) for part in parts_of(pooled, 3)], axis=0)
    embed = dot(pooled, wproj[...])
    embed = embed[:8] + embed[8:16] + embed[16:24]
    for j in range(E // LANES):
        out_ref[:, j, :] = embed[:, j * LANES : (j + 1) * LANES]
    out_ref[:, E // LANES :, :] = jnp.zeros((8, 8 - E // LANES, LANES), F32)


def fetch_kernel(source, query_ref, keys_ref, sems):
    copies = [
        pltpu.make_async_copy(source.at[:, pl.ds(k * D, AHEAD * WIDTH)], target, sems.at[k])
        for k, target in enumerate((query_ref, keys_ref))
    ]
    for copy in copies:
        copy.start()
    for copy in copies:
        copy.wait()


def fetch(w_qkv):
    return pl.pallas_call(
        fetch_kernel,
        out_shape=(pltpu.VMEM((D, AHEAD * WIDTH), BF16),) * 2,
        in_specs=[ANYWHERE],
        out_specs=(IN_VMEM,) * 2,
        scratch_shapes=[pltpu.SemaphoreType.DMA((2,))],
        compiler_params=pltpu.CompilerParams(vmem_limit_bytes=4 << 20),
        cost_estimate=pl.CostEstimate(flops=0, bytes_accessed=4 << 20, transcendentals=0),
        name="fetch",
    )(pltpu.with_memory_space_constraint(w_qkv, pltpu.HBM))


def temporal(x, first, w_qkv, w_out, w_proj):
    return pl.pallas_call(
        temporal_kernel,
        out_shape=pltpu.VMEM((8, 8, LANES), F32),
        in_specs=[IN_VMEM] * 3 + [ANYWHERE] * 3,
        out_specs=IN_VMEM,
        scratch_shapes=[
            pltpu.VMEM((D, 3 * D), BF16),
            pltpu.VMEM((D, D), BF16),
            pltpu.VMEM((D, E), BF16),
            pltpu.SemaphoreType.DMA((16,)),
        ],
        compiler_params=pltpu.CompilerParams(vmem_limit_bytes=30 << 20),
        cost_estimate=pl.CostEstimate(flops=3 << 30, bytes_accessed=11 << 20, transcendentals=0),
        name="temporal",
    )(
        *(pltpu.with_memory_space_constraint(a, pltpu.VMEM) for a in (x, *first)),
        *(pltpu.with_memory_space_constraint(w, pltpu.HBM) for w in (w_qkv, w_out, w_proj)),
    )


def slope(logits, hit):
    sign = jnp.where(hit, 1.0, -1.0)
    return -sign / (1.0 + jnp.exp(sign * logits))


def caption_ids(shape, dimension, rows, gathered):
    spot = lax.broadcasted_iota(jnp.int32, shape, dimension)
    block = spot // rows
    source = lax.axis_index("wide") * jnp.ones(shape, jnp.int32)
    if gathered:
        source = source ^ (block // 8 % 2 * 2) ^ (block // 16) ^ (block // 2 % 4 * 4) ^ (block % 2 * 16)
    return (source * lax.axis_size("narrow") + lax.axis_index("narrow")) * rows + spot % rows


def inverse_lengths(cap):
    ones = jnp.ones((8, E), BF16)
    squares = cap.astype(F32)
    squares = squares * squares
    total = sum(dot_t(ones, part) for part in parts_of(squares, 2))
    return 1.0 / jnp.sqrt(total[:1] + EPS)


def join_kernel(after_ref, *refs):
    rows = refs[0].shape[0]
    for k, ref in enumerate(refs[:-1]):
        refs[-1][k * rows : (k + 1) * rows] = ref[...]


def join(after, arrays):
    rows, columns = arrays[0].shape
    return pl.pallas_call(
        join_kernel,
        out_shape=jax.ShapeDtypeStruct((len(arrays) * rows, columns), arrays[0].dtype),
        in_specs=[ANYWHERE] + [IN_VMEM] * len(arrays),
        out_specs=IN_VMEM,
        compiler_params=pltpu.CompilerParams(vmem_limit_bytes=16 << 20),
        name="join",
    )(after, *arrays)


def unit_kernel(positive_ref, parts_ref, unit_ref, length_ref, send_ref):
    embed = jnp.concatenate(
        [
            jnp.concatenate([parts_ref[2 * c, j : j + 1, :] + parts_ref[2 * c + 1, j : j + 1, :] for j in range(E // LANES)], axis=1)
            for c in range(4)
        ],
        axis=0,
    )
    length = jnp.sqrt(jnp.sum(embed * embed, axis=-1, keepdims=True) + EPS)
    unit = embed / length
    positive = positive_ref[...]
    unit_ref[:, :E] = unit
    unit_ref[:, E:] = positive
    length_ref[...] = jnp.broadcast_to(length, length_ref.shape)
    for k in range(send_ref.shape[0]):
        send_ref[k, :, :E] = unit
        send_ref[k, :, E:] = positive


def make_units(positive, parts, copies):
    return pl.pallas_call(
        unit_kernel,
        out_shape=(
            jax.ShapeDtypeStruct((4, E + LANES), F32),
            jax.ShapeDtypeStruct((4, LANES), F32),
            pltpu.HBM((copies, 4, E + LANES), F32),
        ),
        in_specs=[IN_VMEM, IN_VMEM],
        out_specs=(IN_VMEM,) * 3,
        compiler_params=pltpu.CompilerParams(vmem_limit_bytes=8 << 20),
        name="units",
    )(positive, parts)


def clip_kernel(rows, unit_ref, *refs):
    pieces, grad_ref = refs[:-1], refs[-1]
    terms = jnp.concatenate(parts_of(unit_ref[:, :E], 3), axis=0)
    caps = [ref[...] for ref in pieces]
    scale = TEMP * jnp.concatenate([inverse_lengths(cap) for cap in caps], axis=1)
    logits = jnp.concatenate([dot_t(terms, cap) for cap in caps], axis=1)
    logits = (logits[:4] + logits[4:8] + logits[8:12]) * scale + BIAS
    hit = caption_ids(logits.shape, 1, rows, True).astype(F32) == unit_ref[:, E : E + 1]
    weight = jnp.concatenate(parts_of(slope(logits, hit) * scale, 3), axis=0)
    grad = jnp.zeros((12, E), F32)
    start = 0
    for cap in caps:
        grad += dot(weight[:, start : start + cap.shape[0]], cap)
        start += cap.shape[0]
    grad_ref[...] = grad[:4] + grad[4:8] + grad[8:12]


def clip_part(unit, pieces, rows):
    return pl.pallas_call(
        functools.partial(clip_kernel, rows),
        out_shape=jax.ShapeDtypeStruct((4, E), F32),
        in_specs=[IN_VMEM] * 4,
        out_specs=IN_VMEM,
        compiler_params=pltpu.CompilerParams(vmem_limit_bytes=24 << 20),
        cost_estimate=pl.CostEstimate(flops=100 << 20, bytes_accessed=1 << 20, transcendentals=0),
        name="clip_part",
    )(unit, *pieces)


def caption_sum(cap, length, rows):
    count = cap.shape[0]
    units = parts_of(rows[:, :E], 3)
    positive = rows[:, E:].T[:1]
    logits = sum(dot_t(cap, unit) for unit in units) * (TEMP / length) + BIAS
    ids = caption_ids(logits.shape, 0, count, False).astype(F32)
    weight = jnp.concatenate(parts_of(TEMP * slope(logits, ids == positive), 3), axis=0)
    terms = [dot(weight[: (3 - k) * count], unit) for k, unit in enumerate(units)]
    return sum(term[j * count : (j + 1) * count] for k, term in enumerate(terms) for j in range(3 - k))


def stacked(ref):
    return jnp.concatenate([ref[g] for g in range(ref.shape[0])], axis=0)


def lengths(value):
    return jnp.sqrt(jnp.sum(value * value, axis=-1, keepdims=True) + EPS)


def near_kernel(units_ref, cap_ref, out_ref):
    cap = cap_ref[...]
    out_ref[...] = caption_sum(cap, lengths(cap.astype(F32)), stacked(units_ref))


def last_kernel(units_ref, part_ref, cap_ref, own_ref, along_ref, unit_ref, length_ref, caption_ref, clip_ref):
    unit = unit_ref[:, :E]
    grad = own_ref[...]
    clip_ref[...] = (grad - unit * along_ref[...]) / length_ref[:, :1]
    cap = cap_ref[...]
    value = cap.astype(F32)
    length = lengths(value)
    cap_unit = value / length
    grad = part_ref[...] + caption_sum(cap, length, stacked(units_ref))
    caption_ref[...] = (grad - cap_unit * jnp.sum(cap_unit * grad, axis=-1, keepdims=True)) / length


def swapped(value, axis, bit):
    return lax.ppermute(value, axis, [(i, i ^ bit) for i in range(lax.axis_size(axis))])


def per_device(video, w_qkv, w_out, w_proj, captions, positive):
    wide = lax.axis_size("wide")
    chips = wide // 2
    same_core = [[2 * g + core for g in range(chips)] for core in range(2)]

    send = video.reshape(4, 2, 8, 8, D).transpose(0, 2, 1, 3, 4).reshape(8, 64, D)
    tokens = lax.all_to_all(send, "narrow", 0, 0, tiled=True)

    near = jnp.concatenate([captions, swapped(captions, "wide", 16)], axis=0)
    layers = [near] + [swapped(near, "wide", bit) for bit in (4, 8, 12)]

    parts = temporal(tokens, fetch(w_qkv), w_qkv, w_out, w_proj)
    near = join(parts, layers)
    near = [near, swapped(near, "wide", 2)]
    parts = lax.all_to_all(parts, "narrow", 0, 0, tiled=True)
    pieces = near + [swapped(join(parts, near), "wide", 1)]
    positive = jnp.broadcast_to(positive.astype(F32)[:, None], (4, LANES))
    unit, length, outgoing = make_units(positive, parts, chips)
    grad_unit = clip_part(unit, pieces, captions.shape[0])
    units = lax.all_to_all(outgoing, "wide", 0, 0, axis_index_groups=same_core, tiled=True)
    other = swapped(units, "wide", 1)
    small = pltpu.CompilerParams(vmem_limit_bytes=24 << 20)
    shape = jax.ShapeDtypeStruct(captions.shape, F32)
    part = pl.pallas_call(near_kernel, out_shape=shape, compiler_params=small, name="caption_near")(units, captions)
    others = [swapped(grad_unit, "narrow", bit) for bit in (1, 2, 3)]
    grad_unit = (grad_unit + others[0]) + (others[1] + others[2])
    grad_unit = grad_unit + swapped(grad_unit, "narrow", 4)
    along = jnp.sum(unit[:, :E] * grad_unit, axis=-1, keepdims=True)
    caption_grad, clip_grad = pl.pallas_call(
        last_kernel,
        out_shape=(shape, jax.ShapeDtypeStruct((4, E), F32)),
        compiler_params=small,
        name="gradients",
    )(other, part, captions, grad_unit, along, unit, length)
    return (clip_grad, caption_grad)


def solution(mesh):
    in_specs = (
        P("wide", "narrow", None, None),
        P(),
        P(),
        P(),
        P(("wide", "narrow"), None),
        P("wide"),
    )
    out_specs = (P("wide", None), P(("wide", "narrow"), None))
    return jax.shard_map(
        per_device, mesh=mesh, in_specs=in_specs, out_specs=out_specs, check_vma=False
    )
```
